512 devices in a mesh: seq: 64 (over y, z_lo, core), tp: 8 (over x, z_hi).
Axes of the slice: x: 4, y: 4, z: 16 (z_hi: 2, z_lo: 8; z = z_hi * 8 + z_lo), core: 2. Of those that a mesh axis runs over, the one named last changes fastest.
Arguments:
- tokens: bfloat16 [32768, 2048], P('seq', 'tp'), may hold values from -6 to 6
- w_feature: bfloat16 [2048, 16, 32], P(None, 'tp'), may hold values from -0.125 to 0.125
- w_window: bfloat16 [2048, 16, 384], P(None, 'tp'), may hold values from -0.125 to 0.125
- w_out: bfloat16 [16, 128, 2048], P('tp'), may hold values from -0.125 to 0.125
- win_blocks: int32 [16], P('tp'), may hold values from 1 to 4, as said below
Outputs:
- mixed: bfloat16 [32768, 2048], P(('seq', 'tp'))
The draws below stay inside these ranges and needn't reach their ends.
Inputs may be any that keep to these rules, and one draw needn't show every extreme that they name: `win_blocks`: some head's window spans 4 blocks.
All inputs are finite; a program needn't handle non-finite values.
Results may differ from the reference program's by a relative error of at most 0.017.
Values may be sent and summed in bfloat16 or wider, within the bound.
No kernel may reach another device: no remote copies, remote signals or barrier semaphores. Data moves between devices by JAX's collectives and lax.ppermute only.
A program may use at most 64 MiB of HBM per device.

```python
import math
import jax
import jax.numpy as jnp
from jax import lax

D = 2048
H = 16
HEAD = 128
FEAT = 16
BLOCK = 128
WMAX = 4
TOK_DEV = 512
TOKENS = 32768
HALO = 384
N_TP = 8


def draw_win_blocks(key, part):
    key = jax.random.fold_in(key, 7)
    first_key, second_key = jax.random.split(key)
    spans = jax.random.randint(first_key, (H,), 1, WMAX + 1)
    widest = jax.random.randint(second_key, (), 0, H)
    return jnp.where(jnp.arange(H) == widest, WMAX, spans).astype(jnp.int32)


def level_of(stream_key, dims, shards, smallest, high):
    def one(dim, blocks):
        draws = jax.random.uniform(jax.random.fold_in(jax.random.fold_in(stream_key, 6), dim), (blocks,), jnp.float32, smallest / len(shards), high / len(shards))
        return jnp.repeat(jnp.exp(draws), dims[dim] // blocks).reshape((-1,) + (1,) * (len(dims) - dim - 1))

    gain = one(*shards[0])
    for cut in shards[1:]:
        gain = gain * one(*cut)
    return gain


def scatter_about(stream_key, dims, width, limit, cuts=(), kind=jnp.bfloat16):
    level = level_of(stream_key, dims, cuts, -0.22, 0.18) if cuts else 1.0
    result = jax.random.normal(stream_key, dims, jnp.float32) * width * level
    return jnp.minimum(jnp.maximum(result, -limit), limit).astype(kind)


def setup_inputs(seed: int = 0) -> dict:
    streams_of = jax.random.split(jax.random.key(seed), 6)
    tokens = scatter_about(streams_of[0], (TOKENS, D), 1.0, 6.0, ((0, 64), (1, 8)))
    w_feature = scatter_about(streams_of[1], (D, H, 2 * FEAT), D ** -0.5, 0.125, ((1, 8),))
    w_window = scatter_about(streams_of[2], (D, H, 3 * HEAD), D ** -0.5, 0.125, ((1, 8),))
    w_out = scatter_about(streams_of[3], (H, HEAD, D), (H * HEAD) ** -0.5, 0.125, ((0, 8),))
    win_blocks = draw_win_blocks(jax.random.fold_in(streams_of[5], 71), 0)
    return {"tokens": tokens, "w_feature": w_feature, "w_window": w_window, "w_out": w_out, "win_blocks": win_blocks}


epsilon = 1e-06
score_scale = 12.0
highest = lax.Precision.HIGHEST

def normalize(vector):
    return vector / jnp.sqrt(lax.optimization_barrier(jnp.mean(vector * vector, axis=-1, keepdims=True)) + epsilon)

def taylor(vector):
    outer_prod = (vector[..., :, None] * vector[..., None, :]).reshape(vector.shape[:-1] + (FEAT * FEAT,))
    ones_col = jnp.ones(vector.shape[:-1] + (1,), jnp.float32)
    return jnp.concatenate([ones_col, vector * 0.5, outer_prod * (0.25 / math.sqrt(2.0))], axis=-1)

def reference(tokens, w_feature, w_window, w_out, win_blocks):
    total_rows = tokens.shape[0]
    block_count = total_rows // TOK_DEV
    feature_proj = jnp.dot(tokens, w_feature.reshape(D, H * 2 * FEAT), preferred_element_type=jnp.float32).astype(jnp.bfloat16).reshape(total_rows, H, 2 * FEAT)
    window_proj = jnp.dot(tokens, w_window.reshape(D, H * 3 * HEAD), preferred_element_type=jnp.float32).astype(jnp.bfloat16).reshape(total_rows, H, 3 * HEAD)
    query_feat = feature_proj[..., :FEAT].astype(jnp.float32)
    key_feat = feature_proj[..., FEAT:].astype(jnp.float32)
    values = window_proj[..., 2 * HEAD:]
    values_wide = values.astype(jnp.float32)
    causal = jnp.arange(TOK_DEV)[:, None] >= jnp.arange(TOK_DEV)[None, :]

    def linear_step(state, block_index):
        first_row = (block_index * TOK_DEV).astype(jnp.int32)
        q_block = lax.dynamic_slice_in_dim(query_feat, first_row, TOK_DEV, 0)
        k_block = lax.dynamic_slice_in_dim(key_feat, first_row, TOK_DEV, 0)
        v_block = lax.dynamic_slice_in_dim(values_wide, first_row, TOK_DEV, 0)
        inner_dot = jnp.einsum('thf,uhf->htu', q_block, k_block, precision=highest)
        pair_weight = 1.0 + inner_dot * 0.25 + inner_dot * inner_dot / 32.0
        pair_weight = jnp.where(causal[None], pair_weight, 0.0)
        local_term = jnp.einsum('htu,uhd->thd', pair_weight, v_block, precision=highest)
        carried = jnp.einsum('thf,hfd->thd', taylor(q_block), state, precision=highest)
        new_state = state + jnp.einsum('thf,thd->hfd', taylor(k_block), v_block, precision=highest)
        return (new_state, local_term + carried)
    initial = jnp.zeros((H, 1 + FEAT + FEAT * FEAT, HEAD), jnp.float32)
    final_state, linear_out = lax.scan(linear_step, initial, jnp.arange(block_count).astype(jnp.int32))
    linear_out = linear_out.reshape(total_rows, H, HEAD)
    query_norm = normalize(window_proj[..., :HEAD].astype(jnp.float32)).astype(jnp.bfloat16)
    key_norm = normalize(window_proj[..., HEAD:2 * HEAD].astype(jnp.float32)).astype(jnp.bfloat16)
    front_zeros = jnp.zeros((HALO, H, HEAD), jnp.bfloat16)
    padded_keys = jnp.concatenate([front_zeros, key_norm], axis=0)
    padded_values = jnp.concatenate([front_zeros, values], axis=0)

    def window_block(block_index):
        first_row = (block_index * TOK_DEV).astype(jnp.int32)
        q_block = lax.dynamic_slice_in_dim(query_norm, first_row, TOK_DEV, 0).astype(jnp.float32)
        k_block = lax.dynamic_slice_in_dim(padded_keys, first_row, HALO + TOK_DEV, 0).astype(jnp.float32)
        v_block = lax.dynamic_slice_in_dim(padded_values, first_row, HALO + TOK_DEV, 0).astype(jnp.float32)
        query_pos = first_row + jnp.arange(TOK_DEV).astype(jnp.int32)
        key_pos = first_row - HALO + jnp.arange(HALO + TOK_DEV).astype(jnp.int32)
        scores = jnp.einsum('thd,uhd->htu', q_block, k_block, precision=highest) * (score_scale / HEAD)
        later_key = key_pos[None, None, :]
        allowed = (later_key >= 0) & (later_key <= query_pos[None, :, None]) & (later_key // BLOCK >= query_pos[None, :, None] // BLOCK - win_blocks[:, None, None] + 1)
        weights = jnp.where(allowed, jnp.exp(scores), 0.0).astype(jnp.bfloat16)
        weights = lax.optimization_barrier(weights).astype(jnp.float32)
        return jnp.einsum('htu,uhd->thd', weights, v_block, precision=highest)
    window_out = lax.map(window_block, jnp.arange(block_count).astype(jnp.int32)).reshape(total_rows, H, HEAD)
    hidden = (normalize(linear_out) + normalize(window_out)).astype(jnp.bfloat16)
    group_heads = H // N_TP
    mixed = jnp.zeros((total_rows, D), jnp.float32)
    for group_index in range(N_TP):
        part_heads = hidden[:, group_index * group_heads:(group_index + 1) * group_heads].reshape(total_rows, group_heads * HEAD)
        part_weight = w_out[group_index * group_heads:(group_index + 1) * group_heads].reshape(group_heads * HEAD, D)
        partial_value = jnp.dot(part_heads, part_weight, preferred_element_type=jnp.float32).astype(jnp.bfloat16)
        mixed = mixed + lax.optimization_barrier(partial_value).astype(jnp.float32)
    return mixed.astype(jnp.bfloat16)
```

```python
import jax
import jax.numpy as jnp
import numpy as np
from jax import lax
from jax.sharding import PartitionSpec as P

BLOCK = 128
WMAX = 4
NX, NY, NZ = 4, 4, 8
N_TP = 8
EPS = 1e-06
SCALE = 12.0
bf16, f32 = jnp.bfloat16, jnp.float32


def pairs(move):
    out = []
    for x in range(NX):
        for h in range(2):
            for y in range(NY):
                for z in range(NZ):
                    for c in range(2):
                        to = move(x, h, y, z, c)
                        if to is not None:
                            tx, th, ty, tz, tc = to
                            source = ((y * NZ + z) * 2 + c) * N_TP + x * 2 + h
                            target = ((ty * NZ + tz) * 2 + tc) * N_TP + (tx % NX) * 2 + th
                            out.append((source, target))
    return out


def send(value, move):
    return lax.ppermute(value, ("seq", "tp"), pairs(move))


def to_x(steps):
    return lambda x, h, y, z, c: (x + steps, h, y, z, c)


def to_half(x, h, y, z, c):
    return (x, 1 - h, y, z, c)


def to_core(x, h, y, z, c):
    return (x, h, y, z, 1 - c)


def to_z(flip):
    return lambda x, h, y, z, c: (x, h, y, z ^ flip, c)


def to_y(steps):
    return lambda x, h, y, z, c: (x, h, y + steps, z, c) if y + steps < NY else None


def to_next(x, h, y, z, c):
    place = (y * NZ + z) * 2 + c + 1
    if place == NY * NZ * 2:
        return None
    return (x, h, place // (2 * NZ), place // 2 % NZ, place % 2)


def normalize(vector):
    return vector / jnp.sqrt(jnp.mean(vector * vector, axis=-1, keepdims=True) + EPS)


def feature_maps(feat_dim, rows):
    left = np.zeros((rows, feat_dim), np.float32)
    right = np.zeros((rows, feat_dim), np.float32)
    left_one = np.zeros((rows,), np.float32)
    right_one = np.zeros((rows,), np.float32)
    weight = np.zeros((rows,), np.float32)
    at = 0
    for i in range(feat_dim):
        for j in range(i, feat_dim):
            left[at, i] = 1.0
            right[at, j] = 1.0
            weight[at] = 1.0 / 32.0 if i == j else 1.0 / 16.0
            at += 1
    for i in range(feat_dim):
        left[at, i] = 1.0
        right_one[at] = 1.0
        weight[at] = 0.25
        at += 1
    left_one[at] = right_one[at] = weight[at] = 1.0
    return left, right, left_one, right_one, weight


ROWS = 160


def taylor(vector, maps):
    left, right, left_one, right_one, _ = maps
    a = jnp.einsum("thf,rf->thr", vector, left.astype(bf16), preferred_element_type=f32) + left_one
    b = jnp.einsum("thf,rf->thr", vector, right.astype(bf16), preferred_element_type=f32) + right_one
    return a * b


def prefix(state, place):
    x, h, y, z, c = place
    mine = lax.dynamic_index_in_dim(state, c, 0, False)
    other = lax.dynamic_index_in_dim(state, 1 - c, 0, False)
    got = send(other.astype(bf16), to_core).astype(f32)
    total = mine + got
    short = total.astype(bf16)
    quad = [send(short, to_z(flip)).astype(f32) for flip in (1, 2, 3)]
    before = jnp.zeros_like(total)
    for flip, part in zip((1, 2, 3), quad):
        before = before + jnp.where((z ^ flip) < z, part, 0.0)
        total = total + part
    part = send(total.astype(bf16), to_z(4)).astype(f32)
    before = before + jnp.where((z ^ 4) < z, part, 0.0)
    total = total + part
    short = total.astype(bf16)
    for steps in (1, 2, 3):
        before = before + send(short, to_y(steps)).astype(f32)
    theirs = send((before + jnp.where(c == 0, mine, 0.0)).astype(bf16), to_core).astype(f32)
    ours = before + jnp.where(c == 1, got, 0.0)
    first = jnp.where(c == 0, ours, theirs)
    second = jnp.where(c == 0, theirs, ours)
    return jnp.stack([first, second])


def local(tokens, w_feature, w_window, w_out, win_blocks):
    tok_rows = tokens.shape[0]
    model_width, head_count = w_feature.shape[:2]
    feat_dim = w_feature.shape[2] // 2
    head_size = w_window.shape[2] // 3
    halo_rows = (WMAX - 1) * BLOCK
    seq, tp = lax.axis_index("seq"), lax.axis_index("tp")
    x, h, y, z, c = tp // 2, tp % 2, seq // (2 * NZ), seq // 2 % NZ, seq % 2
    place = (x, h, y, z, c)
    first_row = seq * tok_rows

    other = send(tokens, to_half)
    parts = [tokens] + [send(tokens, to_x(s)) for s in (1, 3, 2)]
    parts += [other] + [send(other, to_x(s)) for s in (1, 3, 2)]
    owners = jnp.stack([(x + NX - s) % NX * 2 + half for half in (h, 1 - h) for s in (0, 1, 3, 2)])

    def ordered(w):
        return jnp.take(w.reshape(N_TP, model_width // N_TP, -1), owners, axis=0)

    window_w = ordered(w_window)
    feature_w = ordered(w_feature)
    stacked = jnp.stack(parts)
    window_sum = jnp.einsum("ktd,kdn->tn", stacked, window_w, preferred_element_type=f32)
    feature_sum = jnp.einsum("ktd,kdn->tn", stacked, feature_w, preferred_element_type=f32)
    window_proj = window_sum.astype(bf16).reshape(tok_rows, head_count, 3 * head_size)
    feature_proj = feature_sum.astype(bf16).reshape(tok_rows, head_count, 2 * feat_dim)
    query_feat, key_feat = feature_proj[..., :feat_dim], feature_proj[..., feat_dim:]
    values = window_proj[..., 2 * head_size :]
    values_wide = values.astype(f32)

    maps = feature_maps(feat_dim, ROWS)
    key_map = taylor(key_feat, maps)
    query_map = taylor(query_feat, maps) * maps[4]
    state = jnp.einsum("thr,thd->hrd", key_map, values_wide, precision=lax.Precision.HIGHEST)
    earlier_state = prefix(state, place)

    key_norm = normalize(window_proj[..., head_size : 2 * head_size].astype(f32)).astype(bf16)
    query_norm = normalize(window_proj[..., :head_size].astype(f32)).astype(bf16)
    key_value = jnp.concatenate([key_norm, values], axis=-1)
    halo = send(key_value[tok_rows - halo_rows :], to_next)

    inner = jnp.einsum("thf,uhf->htu", query_feat, key_feat, preferred_element_type=f32)
    pair_weight = 1.0 + inner * 0.25 + inner * inner / 32.0
    causal = jnp.arange(tok_rows)[:, None] >= jnp.arange(tok_rows)[None, :]
    pair_weight = jnp.where(causal[None], pair_weight, 0.0).astype(bf16)
    local_term = jnp.einsum("htu,uhd->thd", pair_weight, values, preferred_element_type=f32)
    all_keys = jnp.concatenate([halo[..., :head_size], key_norm], axis=0)
    all_values = jnp.concatenate([halo[..., head_size:], values], axis=0)
    scores = jnp.einsum("thd,uhd->htu", query_norm, all_keys, preferred_element_type=f32) * (SCALE / head_size)
    query_pos = first_row + jnp.arange(tok_rows, dtype=jnp.int32)
    key_pos = first_row - halo_rows + jnp.arange(halo_rows + tok_rows, dtype=jnp.int32)
    later_key = key_pos[None, None, :]
    allowed = (
        (later_key >= 0)
        & (later_key <= query_pos[None, :, None])
        & (later_key // BLOCK >= query_pos[None, :, None] // BLOCK - win_blocks[:, None, None] + 1)
    )
    weights = jnp.where(allowed, jnp.exp(scores), 0.0).astype(bf16)
    window_out = jnp.einsum("htu,uhd->thd", weights, all_values, preferred_element_type=f32)

    carried = jnp.einsum("thr,hrd->thd", query_map, earlier_state, precision=lax.Precision.HIGHEST)
    hidden = (normalize(local_term + carried) + normalize(window_out)).astype(bf16)
    hidden = hidden.reshape(tok_rows, head_count * head_size)
    out_cols = w_out.reshape(head_count * head_size, -1)

    rows = hidden.reshape(NX, 2, tok_rows // N_TP, -1)

    def summed(half):
        part = jnp.einsum(
            "xtk,kn->xtn", lax.dynamic_index_in_dim(rows, half, 1, False), out_cols, preferred_element_type=f32
        ).astype(bf16)
        total = lax.dynamic_index_in_dim(part, x, 0, False).astype(f32)
        for steps in (1, 3, 2):
            to = lax.dynamic_index_in_dim(part, (x + steps) % NX, 0, False)
            total = total + send(to, to_x(steps)).astype(f32)
        return total

    away = send(summed(1 - h).astype(bf16), to_half)
    return (summed(h) + away.astype(f32)).astype(bf16)


def solution(mesh):
    in_specs = (P("seq", "tp"), P(None, "tp", None), P(None, "tp", None), P("tp", None, None), P("tp"))
    return jax.shard_map(local, mesh=mesh, in_specs=in_specs, out_specs=P(("seq", "tp"), None), check_vma=False)
```

```python
import jax
import jax.numpy as jnp
import numpy as np
from jax import lax
from jax.experimental import pallas as pl
from jax.experimental.pallas import tpu as pltpu
from jax.sharding import PartitionSpec as P

BLOCK = 128
WMAX = 4
NX, NY, NZ = 4, 4, 8
N_TP = 8
EPS = 1e-06
SCALE = 12.0
bf16, f32 = jnp.bfloat16, jnp.float32


def pairs(move):
    out = []
    for x in range(NX):
        for h in range(2):
            for y in range(NY):
                for z in range(NZ):
                    for c in range(2):
                        to = move(x, h, y, z, c)
                        if to is not None:
                            tx, th, ty, tz, tc = to
                            source = ((y * NZ + z) * 2 + c) * N_TP + x * 2 + h
                            target = ((ty * NZ + tz) * 2 + tc) * N_TP + (tx % NX) * 2 + th
                            out.append((source, target))
    return out


def send(value, move):
    return lax.ppermute(value, ("seq", "tp"), pairs(move))


def to_x(steps):
    return lambda x, h, y, z, c: (x + steps, h, y, z, c)


def to_half(x, h, y, z, c):
    return (x, 1 - h, y, z, c)


def to_core(x, h, y, z, c):
    return (x, h, y, z, 1 - c)


def to_z(flip):
    return lambda x, h, y, z, c: (x, h, y, z ^ flip, c)


def to_y(steps):
    return lambda x, h, y, z, c: (x, h, y + steps, z, c) if y + steps < NY else None


def to_next(x, h, y, z, c):
    place = (y * NZ + z) * 2 + c + 1
    if place == NY * NZ * 2:
        return None
    return (x, h, place // (2 * NZ), place // 2 % NZ, place % 2)


ROWS = 160
VMEM = pl.BlockSpec(memory_space=pltpu.VMEM)
SMEM = pl.BlockSpec(memory_space=pltpu.SMEM)


def feature_maps(feat_dim, heads):
    width = heads * 2 * feat_dim
    tables = np.zeros((heads, 4, ROWS, width), np.float32)
    ones = np.zeros((4, ROWS), np.float32)
    at = 0
    for i in range(feat_dim):
        for j in range(i, feat_dim):
            for head in range(heads):
                query, key = head * 2 * feat_dim, (head * 2 + 1) * feat_dim
                tables[head, 0, at, query + i] = 1.0 / 32.0 if i == j else 1.0 / 16.0
                tables[head, 1, at, query + j] = 1.0
                tables[head, 2, at, key + i] = 1.0
                tables[head, 3, at, key + j] = 1.0
            at += 1
    for i in range(feat_dim):
        for head in range(heads):
            query, key = head * 2 * feat_dim, (head * 2 + 1) * feat_dim
            tables[head, 0, at, query + i] = 0.25
            tables[head, 2, at, key + i] = 1.0
        ones[1, at] = ones[3, at] = 1.0
        at += 1
    ones[:, at] = 1.0
    return tables, ones


def dot(a, b):
    return jnp.dot(a, b, preferred_element_type=f32)


def dot_t(a, b):
    return lax.dot_general(a, b, (((1,), (1,)), ((), ())), preferred_element_type=f32)


def unit(v):
    return v * lax.rsqrt(jnp.mean(v * v, axis=-1, keepdims=True) + EPS)


def halves(v):
    high = v.astype(bf16)
    return high, (v - high.astype(f32)).astype(bf16)


def project_kernel(where, *refs):
    parts = refs[:N_TP]
    wf, ww, table, ones, feats_ref, qn_ref, kv_ref, tail_ref, mine_ref, other_ref = refs[N_TP:]
    core = where[N_TP]
    width = parts[0].shape[1]
    head = ww.shape[2] // 3
    tokens = jnp.concatenate([p[...] for p in parts], axis=1)
    rows = [pl.ds(pl.multiple_of(where[k] * width, width), width) for k in range(N_TP)]

    def columns(pick):
        return dot(tokens, jnp.concatenate([pick(r) for r in rows], axis=0)).astype(bf16)

    feats = columns(lambda r: wf[r, :])
    feats_ref[...] = feats
    first_tail = kv_ref.shape[0] - tail_ref.shape[0]
    states = []
    for kind in (2, 1, 0):
        out = columns(
            lambda r: jnp.concatenate([ww[h, r, kind * head : (kind + 1) * head] for h in range(2)], axis=1)
        )
        if kind == 2:
            kv_ref[:, 2 * head :] = out
            tail_ref[:, 2 * head :] = out[first_tail:]
            for h in range(2):
                left = dot_t(table[h, 2], feats) + ones[2]
                right = dot_t(table[h, 3], feats) + ones[3]
                high, low = halves(left * right)
                v = out[:, h * head : (h + 1) * head]
                states.append(dot(high, v) + dot(low, v))
            mine_ref[...] = jnp.where(core == 0, states[0], states[1])
            other_ref[...] = jnp.where(core == 0, states[1], states[0]).astype(bf16)
            continue
        for h in range(2):
            cols = slice(h * head, (h + 1) * head)
            normed = unit(out[:, cols].astype(f32)).astype(bf16)
            if kind == 1:
                kv_ref[:, cols] = normed
                tail_ref[:, cols] = normed[first_tail:]
            else:
                qn_ref[:, cols] = normed


def local_kernel(where, win, feats_ref, qn_ref, kv_ref, halo_ref, table, ones, near_ref, win_ref, high_ref, low_ref):
    seq = where[0]
    rows = qn_ref.shape[0]
    heads = win_ref.shape[1] // 128
    head = 128
    halo = halo_ref.shape[0]
    span = halo + BLOCK
    feats = feats_ref[...]
    feat = feats.shape[1] // (2 * heads)
    blocks = rows // BLOCK
    row = lax.broadcasted_iota(jnp.int32, (BLOCK, span), 0)
    col = lax.broadcasted_iota(jnp.int32, (BLOCK, span), 1)
    causal = col <= row + halo
    for h in range(heads):
        cols = slice(h * head, (h + 1) * head)
        vcols = slice((heads + h) * head, (heads + h + 1) * head)
        left = dot_t(feats, table[h, 0]) + ones[0:1]
        right = dot_t(feats, table[h, 1]) + ones[1:2]
        high, low = halves(left * right)
        high_ref[h] = high
        low_ref[h] = low
        key = lax.broadcasted_iota(jnp.int32, (feats.shape[1], feats.shape[1]), 0)
        lane = lax.broadcasted_iota(jnp.int32, (feats.shape[1], feats.shape[1]), 1)
        first = h * 2 * feat
        moved = (lane == key + feat) & (key >= first) & (key < first + feat)
        query = dot(feats, jnp.where(moved, 1.0, 0.0).astype(bf16)).astype(bf16)
        keys = jnp.concatenate([halo_ref[:, cols], kv_ref[:, cols]], axis=0)
        values = jnp.concatenate([halo_ref[:, vcols], kv_ref[:, vcols]], axis=0)
        for b in range(blocks):
            at = slice(b * BLOCK, (b + 1) * BLOCK)
            ahead = (b + 1) * BLOCK
            inner = dot_t(query[at], feats[:ahead])
            pair = 1.0 + inner * (0.25 + inner * (1.0 / 32.0))
            last = jnp.where(causal[:, halo:], pair[:, b * BLOCK :], 0.0)
            pair = jnp.concatenate([pair[:, : b * BLOCK], last], axis=1) if b else last
            near_ref[at, cols] = dot(pair.astype(bf16), values[halo : halo + ahead])
            scores = dot_t(qn_ref[at, cols], keys[b * BLOCK : b * BLOCK + span]) * (SCALE / head)
            least = jnp.maximum(span // BLOCK - win[h], span // BLOCK - 1 - (seq * blocks + b))
            allowed = causal & (col >= least * BLOCK)
            weights = jnp.where(allowed, jnp.exp(scores), 0.0).astype(bf16)
            win_ref[at, cols] = unit(dot(weights, values[b * BLOCK : b * BLOCK + span]))


def output_kernel(where, ours, theirs, near_ref, win_ref, high_ref, low_ref, w_ref, *refs):
    outs, hidden = refs[:-1], refs[-1]
    core, x, half = where[0], where[1], where[2]
    mine, other = ours[...], theirs[...].astype(f32)
    head = mine.shape[1]
    rows = hidden.shape[1]
    for h in range(2):
        cols = slice(h * head, (h + 1) * head)
        state_high, state_low = halves(jnp.where(core == h, mine, other))
        high = high_ref[h]
        far = dot(high, state_high) + dot(low_ref[h], state_high) + dot(high, state_low)
        out = (unit(near_ref[:, cols] + far) + win_ref[:, cols]).astype(bf16)
        for g in range(N_TP):
            hidden[g, :, cols] = out[g * rows : (g + 1) * rows]
    weight = w_ref[...]
    for away in (1, 0):
        want = jnp.where(away == 1, 1 - half, half)
        groups = [hidden[lax.rem(x + s, NX) * 2 + want] for s in range(NX)]
        product = dot(jnp.concatenate(groups, axis=0), weight).astype(bf16)
        for s in range(NX):
            outs[(1 - away) * NX + s][...] = product[s * rows : (s + 1) * rows]


def prefix(mine, other, place):
    x, h, y, z, c = place
    got = send(other, to_core).astype(f32)
    total = mine + got
    short = total.astype(bf16)
    quad = [send(short, to_z(flip)).astype(f32) for flip in (1, 2, 3)]
    before = jnp.zeros_like(total)
    for flip, part in zip((1, 2, 3), quad):
        before = before + jnp.where((z ^ flip) < z, part, 0.0)
        total = total + part
    part = send(total.astype(bf16), to_z(4)).astype(f32)
    before = before + jnp.where((z ^ 4) < z, part, 0.0)
    total = total + part
    short = total.astype(bf16)
    for steps in (1, 2, 3):
        before = before + send(short, to_y(steps)).astype(f32)
    theirs = send((before + jnp.where(c == 0, mine, 0.0)).astype(bf16), to_core)
    ours = before + jnp.where(c == 1, got, 0.0)
    return ours, theirs


def shape(dims, kind):
    return jax.ShapeDtypeStruct(dims, kind)


def project(where, parts, wf, ww, tables, ones):
    tok_rows = parts[0].shape[0]
    wide = 2 * ww.shape[2] // 3
    halo_rows = (WMAX - 1) * BLOCK
    return pl.pallas_call(
        project_kernel,
        out_shape=(
            shape((tok_rows, wf.shape[1]), bf16),
            shape((tok_rows, wide), bf16),
            shape((tok_rows, 2 * wide), bf16),
            shape((halo_rows, 2 * wide), bf16),
            shape((ROWS, wide // 2), f32),
            shape((ROWS, wide // 2), bf16),
        ),
        in_specs=[SMEM] + [VMEM] * (N_TP + 4),
        out_specs=(VMEM,) * 6,
        name="project",
        compiler_params=pltpu.CompilerParams(vmem_limit_bytes=LIMIT),
    )(where, *parts, wf, ww, tables.astype(bf16), ones[:, :, None])


def near(where, win_blocks, feats, qn, kv, halo, tables, ones):
    tok_rows, wide = qn.shape
    return pl.pallas_call(
        local_kernel,
        out_shape=(
            shape((tok_rows, wide), f32),
            shape((tok_rows, wide), f32),
            shape((2, tok_rows, ROWS), bf16),
            shape((2, tok_rows, ROWS), bf16),
        ),
        in_specs=[SMEM, SMEM] + [VMEM] * 6,
        out_specs=(VMEM,) * 4,
        name="near",
        compiler_params=pltpu.CompilerParams(vmem_limit_bytes=LIMIT),
    )(where, win_blocks, feats, qn, kv, halo, tables.astype(bf16), ones)


def output(where, ours, theirs, near_out, win_out, high, low, w_out):
    rows = near_out.shape[0] // N_TP
    return pl.pallas_call(
        output_kernel,
        out_shape=(shape((rows, w_out.shape[1]), bf16),) * N_TP,
        in_specs=[SMEM] + [VMEM] * 7,
        out_specs=(VMEM,) * N_TP,
        scratch_shapes=[pltpu.VMEM((N_TP, rows, w_out.shape[0]), bf16)],
        name="output",
        compiler_params=pltpu.CompilerParams(vmem_limit_bytes=LIMIT),
    )(where, ours, theirs, near_out, win_out, high, low, w_out)


LIMIT = 40 * 2**20


def local(tokens, w_feature, w_window, w_out, win_blocks):
    model_width, head_count = w_feature.shape[:2]
    feat_dim = w_feature.shape[2] // 2
    seq, tp = lax.axis_index("seq"), lax.axis_index("tp")
    x, h, y, z, c = tp // 2, tp % 2, seq // (2 * NZ), seq // 2 % NZ, seq % 2

    other = send(tokens, to_half)
    parts = [tokens] + [send(tokens, to_x(s)) for s in (1, 3, 2)]
    parts += [other] + [send(other, to_x(s)) for s in (1, 3, 2)]
    owners = [(x + NX - s) % NX * 2 + half for half in (h, 1 - h) for s in (0, 1, 3, 2)]
    tables, ones = feature_maps(feat_dim, head_count)

    feats, qn, kv, tail, mine, theirs = project(
        jnp.stack(owners + [c]).astype(jnp.int32),
        parts,
        w_feature.reshape(model_width, -1),
        w_window.transpose(1, 0, 2),
        tables,
        ones,
    )
    ours, theirs = prefix(mine, theirs, (x, h, y, z, c))
    halo = send(tail, to_next)
    near_out, win_out, high, low = near(seq[None], win_blocks, feats, qn, kv, halo, tables[:, :2], ones[:2])
    products = output(
        jnp.stack([c, x, h]), ours, theirs, near_out, win_out, high, low, w_out.reshape(-1, model_width)
    )

    def summed(group):
        total = group[0].astype(f32)
        for steps in (1, 3, 2):
            total = total + send(group[steps], to_x(steps)).astype(f32)
        return total

    away = summed(products[:NX]).astype(bf16)
    away, *own = lax.optimization_barrier((away, *products[NX:]))
    away = send(away, to_half)
    return (summed(own) + away.astype(f32)).astype(bf16)


def solution(mesh):
    in_specs = (P("seq", "tp"), P(None, "tp", None), P(None, "tp", None), P("tp", None, None), P("tp"))
    return jax.shard_map(local, mesh=mesh, in_specs=in_specs, out_specs=P(("seq", "tp"), None), check_vma=False)
```

```python
import jax
import jax.numpy as jnp
import numpy as np
from jax import lax
from jax.experimental import pallas as pl
from jax.experimental.pallas import tpu as pltpu
from jax.sharding import PartitionSpec as P

BLOCK = 128
WMAX = 4
NX, NY, NZ = 4, 4, 8
N_TP = 8
EPS = 1e-06
SCALE = 12.0
bf16, f32 = jnp.bfloat16, jnp.float32


def pairs(move):
    out = []
    for x in range(NX):
        for h in range(2):
            for y in range(NY):
                for z in range(NZ):
                    for c in range(2):
                        to = move(x, h, y, z, c)
                        if to is not None:
                            tx, th, ty, tz, tc = to
                            source = ((y * NZ + z) * 2 + c) * N_TP + x * 2 + h
                            target = ((ty * NZ + tz) * 2 + tc) * N_TP + (tx % NX) * 2 + th
                            out.append((source, target))
    return out


def send(value, move):
    return lax.ppermute(value, ("seq", "tp"), pairs(move))


def to_x(steps):
    return lambda x, h, y, z, c: (x + steps, h, y, z, c)


def to_half(x, h, y, z, c):
    return (x, 1 - h, y, z, c)


def to_core(x, h, y, z, c):
    return (x, h, y, z, 1 - c)


def to_z(flip):
    return lambda x, h, y, z, c: (x, h, y, z ^ flip, c)


def to_y(steps):
    return lambda x, h, y, z, c: (x, h, y + steps, z, c) if y + steps < NY else None


def to_next(x, h, y, z, c):
    place = (y * NZ + z) * 2 + c + 1
    if place == NY * NZ * 2:
        return None
    return (x, h, place // (2 * NZ), place // 2 % NZ, place % 2)


ROWS = 160
VMEM = pl.BlockSpec(memory_space=pltpu.VMEM)
SMEM = pl.BlockSpec(memory_space=pltpu.SMEM)


def feature_maps(feat_dim, heads):
    width = heads * 2 * feat_dim
    tables = np.zeros((heads, 4, ROWS, 2 * width), np.float32)
    at = 0
    for i in range(feat_dim):
        for j in range(i, feat_dim):
            for head in range(heads):
                query, key = head * 2 * feat_dim, (head * 2 + 1) * feat_dim
                tables[head, 0, at, query + i] = 1.0 / 32.0 if i == j else 1.0 / 16.0
                tables[head, 1, at, query + j] = 1.0
                tables[head, 2, at, key + i] = 1.0
                tables[head, 3, at, key + j] = 1.0
            at += 1
    for i in range(feat_dim):
        for head in range(heads):
            query, key = head * 2 * feat_dim, (head * 2 + 1) * feat_dim
            tables[head, 0, at, query + i] = 0.25
            tables[head, 2, at, key + i] = 1.0
        tables[:, 1::2, at, width] = 1.0
        at += 1
    tables[:, :, at, width] = 1.0
    return tables


def dot(a, b):
    return jnp.dot(a, b, preferred_element_type=f32)


def dot_t(a, b):
    return lax.dot_general(a, b, (((1,), (1,)), ((), ())), preferred_element_type=f32)


def unit(v):
    return v * lax.rsqrt(jnp.mean(v * v, axis=-1, keepdims=True) + EPS)


def halves(v):
    high = v.astype(bf16)
    return high, (v - high.astype(f32)).astype(bf16)


def position():
    seq, tp = lax.axis_index("seq"), lax.axis_index("tp")
    return lax.div(tp, 2), lax.rem(tp, 2), lax.rem(seq, 2), seq


def project_kernel(*refs):
    parts = refs[:N_TP]
    wf, ww, table, feats_ref, qn_ref, kv_ref, tail_ref, mine_ref, other_ref = refs[N_TP:]
    x, half, core, _ = position()
    owners = [lax.rem(x + NX - s, NX) * 2 + side for side in (half, 1 - half) for s in (0, 1, 3, 2)]
    width = parts[0].shape[1]
    head = ww.shape[2] // 3
    tokens = jnp.concatenate([p[...] for p in parts], axis=1)
    rows = [pl.ds(pl.multiple_of(owner * width, width), width) for owner in owners]

    def columns(pick):
        return dot(tokens, jnp.concatenate([pick(r) for r in rows], axis=0)).astype(bf16)

    feats = columns(lambda r: wf[r, :])
    ones = lax.broadcasted_iota(jnp.int32, feats.shape, 1) == 0
    feats = jnp.concatenate([feats, jnp.where(ones, 1.0, 0.0).astype(bf16)], axis=1)
    feats_ref[...] = feats
    first_tail = kv_ref.shape[0] - tail_ref.shape[0]
    states = []
    for kind in (2, 1, 0):
        out = columns(
            lambda r: jnp.concatenate([ww[h, r, kind * head : (kind + 1) * head] for h in range(2)], axis=1)
        )
        if kind == 2:
            kv_ref[:, 2 * head :] = out
            tail_ref[:, 2 * head :] = out[first_tail:]
            for h in range(2):
                left = dot_t(table[h, 2], feats)
                right = dot_t(table[h, 3], feats)
                high, low = halves(left * right)
                v = out[:, h * head : (h + 1) * head]
                states.append(dot(high, v) + dot(low, v))
            mine_ref[...] = jnp.where(core == 0, states[0], states[1])
            other_ref[...] = jnp.where(core == 0, states[1], states[0]).astype(bf16)
            continue
        for h in range(2):
            cols = slice(h * head, (h + 1) * head)
            normed = unit(out[:, cols].astype(f32)).astype(bf16)
            if kind == 1:
                kv_ref[:, cols] = normed
                tail_ref[:, cols] = normed[first_tail:]
            else:
                qn_ref[:, cols] = normed


def local_kernel(win, feats_ref, qn_ref, kv_ref, halo_ref, table, near_ref, win_ref, high_ref, low_ref):
    seq = position()[3]
    rows = qn_ref.shape[0]
    heads = win_ref.shape[1] // 128
    head = 128
    halo = halo_ref.shape[0]
    span = halo + BLOCK
    feats = feats_ref[...]
    feat = feats.shape[1] // (4 * heads)
    blocks = rows // BLOCK
    row = lax.broadcasted_iota(jnp.int32, (BLOCK, span), 0)
    col = lax.broadcasted_iota(jnp.int32, (BLOCK, span), 1)
    causal = col <= row + halo
    for h in range(heads):
        cols = slice(h * head, (h + 1) * head)
        vcols = slice((heads + h) * head, (heads + h + 1) * head)
        left = dot_t(feats, table[h, 0])
        right = dot_t(feats, table[h, 1])
        high, low = halves(left * right)
        high_ref[h] = high
        low_ref[h] = low
        key = lax.broadcasted_iota(jnp.int32, (feats.shape[1], feats.shape[1]), 0)
        lane = lax.broadcasted_iota(jnp.int32, (feats.shape[1], feats.shape[1]), 1)
        first = h * 2 * feat
        moved = (lane == key + feat) & (key >= first) & (key < first + feat)
        query = dot(feats, jnp.where(moved, 1.0, 0.0).astype(bf16)).astype(bf16)
        keys = jnp.concatenate([halo_ref[:, cols], kv_ref[:, cols]], axis=0)
        values = jnp.concatenate([halo_ref[:, vcols], kv_ref[:, vcols]], axis=0)
        for b in range(blocks):
            at = slice(b * BLOCK, (b + 1) * BLOCK)
            ahead = (b + 1) * BLOCK
            inner = dot_t(query[at], feats[:ahead])
            pair = 1.0 + inner * (0.25 + inner * (1.0 / 32.0))
            last = jnp.where(causal[:, halo:], pair[:, b * BLOCK :], 0.0)
            pair = jnp.concatenate([pair[:, : b * BLOCK], last], axis=1) if b else last
            near_ref[at, cols] = dot(pair.astype(bf16), values[halo : halo + ahead])
            scores = dot_t(qn_ref[at, cols], keys[b * BLOCK : b * BLOCK + span]) * (SCALE / head)
            least = jnp.maximum(span // BLOCK - win[h], span // BLOCK - 1 - (seq * blocks + b))
            allowed = causal & (col >= least * BLOCK)
            weights = jnp.where(allowed, jnp.exp(scores), 0.0).astype(bf16)
            win_ref[at, cols] = unit(dot(weights, values[b * BLOCK : b * BLOCK + span]))


def output_kernel(ours, theirs, near_ref, win_ref, high_ref, low_ref, w_ref, *refs):
    outs, hidden = refs[:-1], refs[-1]
    x, half, core, _ = position()
    mine, other = ours[...], theirs[...].astype(f32)
    head = mine.shape[1]
    rows = hidden.shape[1]
    for h in range(2):
        cols = slice(h * head, (h + 1) * head)
        state_high, state_low = halves(jnp.where(core == h, mine, other))
        high = high_ref[h]
        far = dot(high, state_high) + dot(low_ref[h], state_high) + dot(high, state_low)
        out = (unit(near_ref[:, cols] + far) + win_ref[:, cols]).astype(bf16)
        for g in range(N_TP):
            hidden[g, :, cols] = out[g * rows : (g + 1) * rows]
    weight = w_ref[...]
    for away in (1, 0):
        want = jnp.where(away == 1, 1 - half, half)
        groups = [hidden[lax.rem(x + s, NX) * 2 + want] for s in range(NX)]
        product = dot(jnp.concatenate(groups, axis=0), weight).astype(bf16)
        for s in range(NX):
            outs[(1 - away) * NX + s][...] = product[s * rows : (s + 1) * rows]


def prefix(mine, other, place, beside):
    x, h, y, z, c = place
    got = send(other, to_core).astype(f32)
    total = mine + got
    before = jnp.zeros_like(total)
    done = None
    for flip in (1, 2, 4):
        part = send(total.astype(bf16), to_z(flip)).astype(f32)
        before = before + jnp.where((z ^ flip) < z, part, 0.0)
        total = total + part
        if flip == 1:
            done = beside(total)
    total, done = lax.optimization_barrier((total, done))
    short = total.astype(bf16)
    for steps in (1, 2, 3):
        before = before + send(short, to_y(steps)).astype(f32)
    theirs = send((before + jnp.where(c == 0, mine, 0.0)).astype(bf16), to_core)
    ours = before + jnp.where(c == 1, got, 0.0)
    return ours, theirs, done


def shape(dims, kind):
    return jax.ShapeDtypeStruct(dims, kind)


def project(parts, wf, ww, tables):
    tok_rows = parts[0].shape[0]
    wide = 2 * ww.shape[2] // 3
    halo_rows = (WMAX - 1) * BLOCK
    return pl.pallas_call(
        project_kernel,
        out_shape=(
            shape((tok_rows, 2 * wf.shape[1]), bf16),
            shape((tok_rows, wide), bf16),
            shape((tok_rows, 2 * wide), bf16),
            shape((halo_rows, 2 * wide), bf16),
            shape((ROWS, wide // 2), f32),
            shape((ROWS, wide // 2), bf16),
        ),
        in_specs=[VMEM] * (N_TP + 3),
        out_specs=(VMEM,) * 6,
        name="project",
        compiler_params=pltpu.CompilerParams(vmem_limit_bytes=LIMIT),
    )(*parts, wf, ww, tables.astype(bf16))


def near(win_blocks, feats, qn, kv, halo, tables):
    tok_rows, wide = qn.shape
    return pl.pallas_call(
        local_kernel,
        out_shape=(
            shape((tok_rows, wide), f32),
            shape((tok_rows, wide), f32),
            shape((2, tok_rows, ROWS), bf16),
            shape((2, tok_rows, ROWS), bf16),
        ),
        in_specs=[SMEM] + [VMEM] * 5,
        out_specs=(VMEM,) * 4,
        name="near",
        compiler_params=pltpu.CompilerParams(vmem_limit_bytes=LIMIT),
    )(win_blocks, feats, qn, kv, halo, tables.astype(bf16))


def output(ours, theirs, near_out, win_out, high, low, w_out):
    rows = near_out.shape[0] // N_TP
    return pl.pallas_call(
        output_kernel,
        out_shape=(shape((rows, w_out.shape[1]), bf16),) * N_TP,
        in_specs=[VMEM] * 7,
        out_specs=(VMEM,) * N_TP,
        scratch_shapes=[pltpu.VMEM((N_TP, rows, w_out.shape[0]), bf16)],
        name="output",
        compiler_params=pltpu.CompilerParams(vmem_limit_bytes=LIMIT),
    )(ours, theirs, near_out, win_out, high, low, w_out)


LIMIT = 16 * 2**20


def local(tokens, w_feature, w_window, w_out, win_blocks):
    model_width, head_count = w_feature.shape[:2]
    feat_dim = w_feature.shape[2] // 2
    seq, tp = lax.axis_index("seq"), lax.axis_index("tp")
    x, h, y, z, c = tp // 2, tp % 2, seq // (2 * NZ), seq // 2 % NZ, seq % 2

    other = send(tokens, to_half)
    parts = [tokens] + [send(tokens, to_x(s)) for s in (1, 3, 2)]
    parts += [other] + [send(other, to_x(s)) for s in (1, 3, 2)]
    tables = feature_maps(feat_dim, head_count)
    feats, qn, kv, tail, mine, theirs = project(
        parts, w_feature.reshape(model_width, -1), w_window.transpose(1, 0, 2), tables
    )

    def beside(total):
        halo, _ = lax.optimization_barrier((send(tail, to_next), total))
        return near(win_blocks, feats, qn, kv, halo, tables[:, :2])

    ours, theirs, attended = prefix(mine, theirs, (x, h, y, z, c), beside)
    products = output(ours, theirs, *attended, w_out.reshape(-1, model_width))

    def summed(group):
        total = group[0].astype(f32)
        for steps in (1, 3, 2):
            total = total + send(group[steps], to_x(steps)).astype(f32)
        return total

    away = summed(products[:NX]).astype(bf16)
    away, *own = lax.optimization_barrier((away, *products[NX:]))
    away = send(away, to_half)
    return (summed(own) + away.astype(f32)).astype(bf16)


def solution(mesh):
    in_specs = (P("seq", "tp"), P(None, "tp", None), P(None, "tp", None), P("tp", None, None), P("tp"))
    return jax.shard_map(local, mesh=mesh, in_specs=in_specs, out_specs=P(("seq", "tp"), None), check_vma=False)
```

```python
import jax
import jax.numpy as jnp
import numpy as np
from jax import lax
from jax.experimental import pallas as pl
from jax.experimental.pallas import tpu as pltpu
from jax.sharding import PartitionSpec as P

BLOCK = 128
WMAX = 4
NX, NY, NZ = 4, 4, 8
N_TP = 8
EPS = 1e-06
SCALE = 12.0
bf16, f32 = jnp.bfloat16, jnp.float32


def pairs(move):
    out = []
    for x in range(NX):
        for h in range(2):
            for y in range(NY):
                for z in range(NZ):
                    for c in range(2):
                        to = move(x, h, y, z, c)
                        if to is not None:
                            tx, th, ty, tz, tc = to
                            source = ((y * NZ + z) * 2 + c) * N_TP + x * 2 + h
                            target = ((ty * NZ + tz) * 2 + tc) * N_TP + (tx % NX) * 2 + th
                            out.append((source, target))
    return out


def send(value, move):
    return lax.ppermute(value, ("seq", "tp"), pairs(move))


def to_x(steps):
    return lambda x, h, y, z, c: (x + steps, h, y, z, c)


def to_half(x, h, y, z, c):
    return (x, 1 - h, y, z, c)


def to_core(x, h, y, z, c):
    return (x, h, y, z, 1 - c)


def to_z(flip):
    return lambda x, h, y, z, c: (x, h, y, z ^ flip, c)


def to_y(steps):
    return lambda x, h, y, z, c: (x, h, y + steps, z, c) if y + steps < NY else None


def to_next(x, h, y, z, c):
    place = (y * NZ + z) * 2 + c + 1
    if place == NY * NZ * 2:
        return None
    return (x, h, place // (2 * NZ), place // 2 % NZ, place % 2)


ROWS = 160
VMEM = pl.BlockSpec(memory_space=pltpu.VMEM)
ANY = pl.BlockSpec(memory_space=pl.ANY)
SMEM = pl.BlockSpec(memory_space=pltpu.SMEM)


def feature_maps(feat_dim, heads):
    width = heads * 2 * feat_dim
    tables = np.zeros((heads, 4, ROWS, 2 * width), np.float32)
    at = 0
    for i in range(feat_dim):
        for j in range(i, feat_dim):
            for head in range(heads):
                query, key = head * 2 * feat_dim, (head * 2 + 1) * feat_dim
                tables[head, 0, at, query + i] = 1.0 / 32.0 if i == j else 1.0 / 16.0
                tables[head, 1, at, query + j] = 1.0
                tables[head, 2, at, key + i] = 1.0
                tables[head, 3, at, key + j] = 1.0
            at += 1
    for i in range(feat_dim):
        for head in range(heads):
            query, key = head * 2 * feat_dim, (head * 2 + 1) * feat_dim
            tables[head, 0, at, query + i] = 0.25
            tables[head, 2, at, key + i] = 1.0
        tables[:, 1::2, at, width] = 1.0
        at += 1
    tables[:, :, at, width] = 1.0
    return tables


def dot(a, b):
    return jnp.dot(a, b, preferred_element_type=f32)


def dot_t(a, b):
    return lax.dot_general(a, b, (((1,), (1,)), ((), ())), preferred_element_type=f32)


def unit(v):
    return v * lax.rsqrt(jnp.mean(v * v, axis=-1, keepdims=True) + EPS)


def halves(v):
    high = v.astype(bf16)
    return high, (v - high.astype(f32)).astype(bf16)


def position():
    seq, tp = lax.axis_index("seq"), lax.axis_index("tp")
    return lax.div(tp, 2), lax.rem(tp, 2), lax.rem(seq, 2), seq


def project_kernel(*refs):
    parts = refs[:N_TP]
    wf, ww, table, feats_ref, qn_ref, kv_ref, tail_ref, mine_ref, other_ref, held, sems = refs[N_TP:]
    x, half, core, _ = position()
    owners = [lax.rem(x + NX - s, NX) * 2 + side for side in (half, 1 - half) for s in (0, 1, 3, 2)]
    width = parts[0].shape[1]
    head = ww.shape[2] // 3
    copies = [
        pltpu.make_async_copy(part, held.at[:, pl.ds(pl.multiple_of(owner * width, width), width)], sems.at[k])
        for k, (part, owner) in enumerate(zip(parts, owners))
    ]
    for copy in copies:
        copy.start()
    for copy in copies:
        copy.wait()
    tokens = held[...]

    def columns(weight):
        return dot(tokens, weight).astype(bf16)

    feats = columns(wf[...])
    ones = lax.broadcasted_iota(jnp.int32, feats.shape, 1) == 0
    feats = jnp.concatenate([feats, jnp.where(ones, 1.0, 0.0).astype(bf16)], axis=1)
    feats_ref[...] = feats
    first_tail = kv_ref.shape[0] - tail_ref.shape[0]
    states = []
    for kind in (2, 1, 0):
        out = columns(jnp.concatenate([ww[h, :, kind * head : (kind + 1) * head] for h in range(2)], axis=1))
        if kind == 2:
            kv_ref[:, 2 * head :] = out
            tail_ref[:, 2 * head :] = out[first_tail:]
            for h in range(2):
                left = dot_t(table[h, 2], feats)
                right = dot_t(table[h, 3], feats)
                high, low = halves(left * right)
                v = out[:, h * head : (h + 1) * head]
                states.append(dot(high, v) + dot(low, v))
            mine_ref[...] = jnp.where(core == 0, states[0], states[1])
            other_ref[...] = jnp.where(core == 0, states[1], states[0]).astype(bf16)
            continue
        for h in range(2):
            cols = slice(h * head, (h + 1) * head)
            normed = unit(out[:, cols].astype(f32)).astype(bf16)
            if kind == 1:
                kv_ref[:, cols] = normed
                tail_ref[:, cols] = normed[first_tail:]
            else:
                qn_ref[:, cols] = normed


def local_kernel(win, feats_ref, qn_ref, kv_ref, halo_ref, table, near_ref, win_ref, high_ref, low_ref):
    seq = position()[3]
    rows = qn_ref.shape[0]
    heads = win_ref.shape[1] // 128
    head = 128
    halo = halo_ref.shape[0]
    span = halo + BLOCK
    feats = feats_ref[...]
    feat = feats.shape[1] // (4 * heads)
    blocks = rows // BLOCK
    row = lax.broadcasted_iota(jnp.int32, (BLOCK, span), 0)
    col = lax.broadcasted_iota(jnp.int32, (BLOCK, span), 1)
    causal = col <= row + halo
    for h in range(heads):
        cols = slice(h * head, (h + 1) * head)
        vcols = slice((heads + h) * head, (heads + h + 1) * head)
        left = dot_t(feats, table[h, 0])
        right = dot_t(feats, table[h, 1])
        high, low = halves(left * right)
        high_ref[h] = high
        low_ref[h] = low
        key = lax.broadcasted_iota(jnp.int32, (feats.shape[1], feats.shape[1]), 0)
        lane = lax.broadcasted_iota(jnp.int32, (feats.shape[1], feats.shape[1]), 1)
        first = h * 2 * feat
        moved = (lane == key + feat) & (key >= first) & (key < first + feat)
        query = dot(feats, jnp.where(moved, 1.0, 0.0).astype(bf16)).astype(bf16)
        keys = jnp.concatenate([halo_ref[:, cols], kv_ref[:, cols]], axis=0)
        values = jnp.concatenate([halo_ref[:, vcols], kv_ref[:, vcols]], axis=0)
        for b in range(blocks):
            at = slice(b * BLOCK, (b + 1) * BLOCK)
            ahead = (b + 1) * BLOCK
            inner = dot_t(query[at], feats[:ahead])
            pair = 1.0 + inner * (0.25 + inner * (1.0 / 32.0))
            last = jnp.where(causal[:, halo:], pair[:, b * BLOCK :], 0.0)
            pair = jnp.concatenate([pair[:, : b * BLOCK], last], axis=1) if b else last
            near_ref[at, cols] = dot(pair.astype(bf16), values[halo : halo + ahead])
            scores = dot_t(qn_ref[at, cols], keys[b * BLOCK : b * BLOCK + span]) * (SCALE / head)
            least = jnp.maximum(span // BLOCK - win[h], span // BLOCK - 1 - (seq * blocks + b))
            allowed = causal & (col >= least * BLOCK)
            weights = jnp.where(allowed, jnp.exp(scores), 0.0).astype(bf16)
            win_ref[at, cols] = unit(dot(weights, values[b * BLOCK : b * BLOCK + span]))


def hidden_kernel(ours, theirs, near_ref, win_ref, high_ref, low_ref, keep_ref, away_ref, hidden):
    x, half, core, _ = position()
    mine, other = ours[...], theirs[...].astype(f32)
    head = mine.shape[1]
    rows = hidden.shape[1]
    for h in range(2):
        cols = slice(h * head, (h + 1) * head)
        state_high, state_low = halves(jnp.where(core == h, mine, other))
        high = high_ref[h]
        far = dot(high, state_high) + dot(low_ref[h], state_high) + dot(high, state_low)
        out = (unit(near_ref[:, cols] + far) + win_ref[:, cols]).astype(bf16)
        for g in range(N_TP):
            hidden[g, :, cols] = out[g * rows : (g + 1) * rows]
    for s in range(NX):
        group = lax.rem(x + s, NX) * 2
        keep_ref[s * rows : (s + 1) * rows] = hidden[group + half]
        away_ref[s * rows : (s + 1) * rows] = hidden[group + 1 - half]


def product_kernel(keep_ref, got_ref, w_ref, w_got_ref, *outs):
    rows = outs[0].shape[0]
    product = (dot(keep_ref[...], w_ref[...]) + dot(got_ref[...], w_got_ref[...])).astype(bf16)
    for s, out in enumerate(outs):
        out[...] = product[s * rows : (s + 1) * rows]


def prefix(mine, other, place, beside):
    x, h, y, z, c = place
    got = send(other, to_core).astype(f32)
    total = mine + got
    before = jnp.zeros_like(total)
    done = None
    for flip in (1, 2, 4):
        part = send(total.astype(bf16), to_z(flip))
        if flip == 4:
            part, done = lax.optimization_barrier((part, done))
        part = part.astype(f32)
        before = before + jnp.where((z ^ flip) < z, part, 0.0)
        total = total + part
        if flip == 1:
            done = beside(total)
    short = total.astype(bf16)
    for steps in (1, 2, 3):
        before = before + send(short, to_y(steps)).astype(f32)
    theirs = send((before + jnp.where(c == 0, mine, 0.0)).astype(bf16), to_core)
    ours = before + jnp.where(c == 1, got, 0.0)
    return ours, theirs, done


def shape(dims, kind):
    return jax.ShapeDtypeStruct(dims, kind)


def project(parts, wf, ww, tables):
    tok_rows = parts[0].shape[0]
    wide = 2 * ww.shape[2] // 3
    halo_rows = (WMAX - 1) * BLOCK
    return pl.pallas_call(
        project_kernel,
        out_shape=(
            shape((tok_rows, 2 * wf.shape[1]), bf16),
            shape((tok_rows, wide), bf16),
            shape((tok_rows, 2 * wide), bf16),
            shape((halo_rows, 2 * wide), bf16),
            shape((ROWS, wide // 2), f32),
            shape((ROWS, wide // 2), bf16),
        ),
        in_specs=[ANY] * N_TP + [VMEM] * 3,
        out_specs=(VMEM,) * 6,
        scratch_shapes=[pltpu.VMEM((tok_rows, wf.shape[0]), bf16), pltpu.SemaphoreType.DMA((N_TP,))],
        name="project",
        compiler_params=pltpu.CompilerParams(vmem_limit_bytes=LIMIT),
    )(*parts, wf, ww, tables.astype(bf16))


def near(win_blocks, feats, qn, kv, halo, tables):
    tok_rows, wide = qn.shape
    return pl.pallas_call(
        local_kernel,
        out_shape=(
            shape((tok_rows, wide), f32),
            shape((tok_rows, wide), f32),
            shape((2, tok_rows, ROWS), bf16),
            shape((2, tok_rows, ROWS), bf16),
        ),
        in_specs=[SMEM] + [VMEM] * 5,
        out_specs=(VMEM,) * 4,
        name="near",
        compiler_params=pltpu.CompilerParams(vmem_limit_bytes=LIMIT),
    )(win_blocks, feats, qn, kv, halo, tables.astype(bf16))


def hidden_rows(ours, theirs, near_out, win_out, high, low):
    tok_rows, wide = near_out.shape
    return pl.pallas_call(
        hidden_kernel,
        out_shape=(shape((tok_rows // 2, wide), bf16),) * 2,
        in_specs=[VMEM] * 6,
        out_specs=(VMEM,) * 2,
        scratch_shapes=[pltpu.VMEM((N_TP, tok_rows // N_TP, wide), bf16)],
        name="hidden",
        compiler_params=pltpu.CompilerParams(vmem_limit_bytes=LIMIT),
    )(ours, theirs, near_out, win_out, high, low)


def product(keep, got, w_out, w_got):
    return pl.pallas_call(
        product_kernel,
        out_shape=(shape((keep.shape[0] // NX, w_out.shape[1]), bf16),) * NX,
        in_specs=[VMEM] * 4,
        out_specs=(VMEM,) * NX,
        name="product",
        compiler_params=pltpu.CompilerParams(vmem_limit_bytes=LIMIT),
    )(keep, got, w_out, w_got)


LIMIT = 16 * 2**20


def local(tokens, w_feature, w_window, w_out, win_blocks):
    model_width, head_count = w_feature.shape[:2]
    feat_dim = w_feature.shape[2] // 2
    seq, tp = lax.axis_index("seq"), lax.axis_index("tp")
    x, h, y, z, c = tp // 2, tp % 2, seq // (2 * NZ), seq // 2 % NZ, seq % 2

    other = send(tokens, to_half)
    parts = [tokens] + [send(tokens, to_x(s)) for s in (1, 3, 2)]
    w_out = w_out.reshape(-1, model_width)
    piece_rows = w_out.shape[0] // (2 * NY)
    piece = lax.dynamic_slice_in_dim(w_out, (y * 2 + c) * piece_rows, piece_rows, 0)
    other, piece = lax.optimization_barrier((other, piece))
    parts += [other] + [send(other, to_x(s)) for s in (1, 3, 2)]
    piece = send(piece, to_half)
    tables = feature_maps(feat_dim, head_count)
    feats, qn, kv, tail, mine, theirs = project(
        parts, w_feature.reshape(model_width, -1), w_window.transpose(1, 0, 2), tables
    )

    def beside(total):
        halo, _ = lax.optimization_barrier((send(tail, to_next), total))
        return near(win_blocks, feats, qn, kv, halo, tables[:, :2])

    mine, piece = lax.optimization_barrier((mine, piece))
    alike = [[(row * NZ + at) * 2 + core for row in range(NY) for core in range(2)] for at in range(NZ)]
    w_got = lax.all_gather(piece, "seq", axis=0, axis_index_groups=alike, tiled=True)
    ours, theirs, attended = prefix(mine, theirs, (x, h, y, z, c), beside)
    keep, away = hidden_rows(ours, theirs, *attended)
    products = product(keep, send(away, to_half), w_out, w_got)
    total = products[0].astype(f32)
    for steps in (1, 3, 2):
        total = total + send(products[steps], to_x(steps)).astype(f32)
    return total.astype(bf16)


def solution(mesh):
    in_specs = (P("seq", "tp"), P(None, "tp", None), P(None, "tp", None), P("tp", None, None), P("tp"))
    return jax.shard_map(local, mesh=mesh, in_specs=in_specs, out_specs=P(("seq", "tp"), None), check_vma=False)
```

```python
import jax
import jax.numpy as jnp
import numpy as np
from jax import lax
from jax.experimental import pallas as pl
from jax.experimental.pallas import tpu as pltpu
from jax.sharding import PartitionSpec as P

BLOCK = 128
WMAX = 4
NX, NY, NZ = 4, 4, 8
N_TP = 8
EPS = 1e-06
SCALE = 12.0
bf16, f32 = jnp.bfloat16, jnp.float32


def pairs(move):
    out = []
    for x in range(NX):
        for h in range(2):
            for y in range(NY):
                for z in range(NZ):
                    for c in range(2):
                        to = move(x, h, y, z, c)
                        if to is not None:
                            tx, th, ty, tz, tc = to
                            source = ((y * NZ + z) * 2 + c) * N_TP + x * 2 + h
                            target = ((ty * NZ + tz) * 2 + tc) * N_TP + (tx % NX) * 2 + th
                            out.append((source, target))
    return out


def send(value, move):
    return lax.ppermute(value, ("seq", "tp"), pairs(move))


def to_x(steps):
    return lambda x, h, y, z, c: (x + steps, h, y, z, c)


def to_half(x, h, y, z, c):
    return (x, 1 - h, y, z, c)


def to_core(x, h, y, z, c):
    return (x, h, y, z, 1 - c)


def to_z(flip):
    return lambda x, h, y, z, c: (x, h, y, z ^ flip, c)


def to_y(steps):
    return lambda x, h, y, z, c: (x, h, y + steps, z, c) if y + steps < NY else None


def to_next(x, h, y, z, c):
    place = (y * NZ + z) * 2 + c + 1
    if place == NY * NZ * 2:
        return None
    return (x, h, place // (2 * NZ), place // 2 % NZ, place % 2)


ROWS = 160
VMEM = pl.BlockSpec(memory_space=pltpu.VMEM)
HBM = pl.BlockSpec(memory_space=pltpu.HBM)
SMEM = pl.BlockSpec(memory_space=pltpu.SMEM)


def feature_maps(feat_dim, heads):
    width = heads * 2 * feat_dim
    tables = np.zeros((heads, 4, ROWS, 2 * width), np.float32)
    at = 0
    for i in range(feat_dim):
        for j in range(i, feat_dim):
            for head in range(heads):
                query, key = head * 2 * feat_dim, (head * 2 + 1) * feat_dim
                tables[head, 0, at, query + i] = 1.0 / 32.0 if i == j else 1.0 / 16.0
                tables[head, 1, at, query + j] = 1.0
                tables[head, 2, at, key + i] = 1.0
                tables[head, 3, at, key + j] = 1.0
            at += 1
    for i in range(feat_dim):
        for head in range(heads):
            query, key = head * 2 * feat_dim, (head * 2 + 1) * feat_dim
            tables[head, 0, at, query + i] = 0.25
            tables[head, 2, at, key + i] = 1.0
        tables[:, 1::2, at, width] = 1.0
        at += 1
    tables[:, :, at, width] = 1.0
    return tables


def dot(a, b):
    return jnp.dot(a, b, preferred_element_type=f32)


def dot_t(a, b):
    return lax.dot_general(a, b, (((1,), (1,)), ((), ())), preferred_element_type=f32)


def unit(v):
    return v * lax.rsqrt(jnp.mean(v * v, axis=-1, keepdims=True) + EPS)


def halves(v):
    high = v.astype(bf16)
    return high, (v - high.astype(f32)).astype(bf16)


def position():
    seq, tp = lax.axis_index("seq"), lax.axis_index("tp")
    return lax.div(tp, 2), lax.rem(tp, 2), lax.rem(seq, 2), seq


def project_kernel(*refs):
    parts = refs[:N_TP]
    wf, ww, table, qf_ref, kv_ref, tail_ref, mine_ref, other_ref, held, held_wf, qf, tail, sems = refs[N_TP:]
    x, half, core, _ = position()
    owners = [lax.rem(x + NX - s, NX) * 2 + side for side in (half, 1 - half) for s in (0, 1, 3, 2)]
    width = parts[0].shape[1]
    head = ww.shape[2] // 3
    copies = [
        pltpu.make_async_copy(part, held.at[:, pl.ds(pl.multiple_of(owner * width, width), width)], sems.at[k])
        for k, (part, owner) in enumerate(zip(parts, owners))
    ]
    copies.append(pltpu.make_async_copy(wf, held_wf, sems.at[N_TP]))
    for copy in copies:
        copy.start()
    for copy in copies:
        copy.wait()
    tokens = held[...]

    def columns(weight):
        return dot(tokens, weight).astype(bf16)

    feats = columns(held_wf[...])
    ones = lax.broadcasted_iota(jnp.int32, feats.shape, 1) == 0
    feats = jnp.concatenate([feats, jnp.where(ones, 1.0, 0.0).astype(bf16)], axis=1)
    qf[:, 2 * head :] = feats
    first_tail = kv_ref.shape[0] - tail.shape[0]
    leave = [pltpu.make_async_copy(tail, tail_ref, sems.at[0]), pltpu.make_async_copy(qf, qf_ref, sems.at[1])]
    for kind in (2, 1, 0):
        out = columns(jnp.concatenate([ww[h, :, kind * head : (kind + 1) * head] for h in range(2)], axis=1))
        if kind == 2:
            values = out
            kv_ref[:, 2 * head :] = out
            tail[:, 2 * head :] = out[first_tail:]
            continue
        for h in range(2):
            cols = slice(h * head, (h + 1) * head)
            normed = unit(out[:, cols].astype(f32)).astype(bf16)
            if kind == 1:
                kv_ref[:, cols] = normed
                tail[:, cols] = normed[first_tail:]
            else:
                qf[:, cols] = normed
        leave[1 - kind].start()
    states = []
    for h in range(2):
        left = dot_t(table[h, 2], feats)
        right = dot_t(table[h, 3], feats)
        high, low = halves(left * right)
        v = values[:, h * head : (h + 1) * head]
        states.append(dot(high, v) + dot(low, v))
    mine_ref[...] = jnp.where(core == 0, states[0], states[1])
    other_ref[...] = jnp.where(core == 0, states[1], states[0]).astype(bf16)
    for copy in leave:
        copy.wait()


def local_kernel(win, qf_ref, kv_ref, halo_ref, table, near_ref, win_ref, high_ref, low_ref, qn_ref, sem):
    copy = pltpu.make_async_copy(qf_ref, qn_ref, sem)
    copy.start()
    copy.wait()
    seq = position()[3]
    rows = qn_ref.shape[0]
    heads = win_ref.shape[1] // 128
    head = 128
    halo = halo_ref.shape[0]
    span = halo + BLOCK
    feats = qn_ref[:, heads * head :]
    feat = feats.shape[1] // (4 * heads)
    blocks = rows // BLOCK
    row = lax.broadcasted_iota(jnp.int32, (BLOCK, span), 0)
    col = lax.broadcasted_iota(jnp.int32, (BLOCK, span), 1)
    causal = col <= row + halo
    for h in range(heads):
        cols = slice(h * head, (h + 1) * head)
        vcols = slice((heads + h) * head, (heads + h + 1) * head)
        left = dot_t(feats, table[h, 0])
        right = dot_t(feats, table[h, 1])
        high, low = halves(left * right)
        high_ref[h] = high
        low_ref[h] = low
        key = lax.broadcasted_iota(jnp.int32, (feats.shape[1], feats.shape[1]), 0)
        lane = lax.broadcasted_iota(jnp.int32, (feats.shape[1], feats.shape[1]), 1)
        first = h * 2 * feat
        moved = (lane == key + feat) & (key >= first) & (key < first + feat)
        query = dot(feats, jnp.where(moved, 1.0, 0.0).astype(bf16)).astype(bf16)
        keys = jnp.concatenate([halo_ref[:, cols], kv_ref[:, cols]], axis=0)
        values = jnp.concatenate([halo_ref[:, vcols], kv_ref[:, vcols]], axis=0)
        for b in range(blocks):
            at = slice(b * BLOCK, (b + 1) * BLOCK)
            ahead = (b + 1) * BLOCK
            inner = dot_t(query[at], feats[:ahead])
            pair = 1.0 + inner * (0.25 + inner * (1.0 / 32.0))
            last = jnp.where(causal[:, halo:], pair[:, b * BLOCK :], 0.0)
            pair = jnp.concatenate([pair[:, : b * BLOCK], last], axis=1) if b else last
            near_ref[at, cols] = dot(pair.astype(bf16), values[halo : halo + ahead])
            scores = dot_t(qn_ref[at, cols], keys[b * BLOCK : b * BLOCK + span]) * (SCALE / head)
            least = jnp.maximum(span // BLOCK - win[h], span // BLOCK - 1 - (seq * blocks + b))
            allowed = causal & (col >= least * BLOCK)
            weights = jnp.where(allowed, jnp.exp(scores), 0.0).astype(bf16)
            win_ref[at, cols] = unit(dot(weights, values[b * BLOCK : b * BLOCK + span]))


def hidden_kernel(ours, theirs, near_ref, win_ref, high_ref, low_ref, keep_ref, away_ref, hidden):
    x, half, core, _ = position()
    mine, other = ours[...], theirs[...].astype(f32)
    head = mine.shape[1]
    rows = hidden.shape[1]
    for h in range(2):
        cols = slice(h * head, (h + 1) * head)
        state_high, state_low = halves(jnp.where(core == h, mine, other))
        high = high_ref[h]
        far = dot(high, state_high) + dot(low_ref[h], state_high) + dot(high, state_low)
        out = (unit(near_ref[:, cols] + far) + win_ref[:, cols]).astype(bf16)
        for g in range(N_TP):
            hidden[g, :, cols] = out[g * rows : (g + 1) * rows]
    for s in range(NX):
        group = lax.rem(x + s, NX) * 2
        keep_ref[s * rows : (s + 1) * rows] = hidden[group + half]
        away_ref[s * rows : (s + 1) * rows] = hidden[group + 1 - half]


def product_kernel(hidden_ref, w_ref, *outs):
    rows = outs[0].shape[0]
    product = dot(hidden_ref[...], w_ref[...]).astype(bf16)
    for s, out in enumerate(outs):
        out[...] = product[s * rows : (s + 1) * rows]


def prefix(mine, other, place, halo, beside):
    x, h, y, z, c = place
    got = send(other, to_core).astype(f32)
    total = mine + got
    add = (jnp.where(c == 0, mine, 0.0), jnp.where(c == 1, got, 0.0))
    total, add = lax.optimization_barrier((total, add))
    before = jnp.zeros_like(total)
    done = None
    for flip in (1, 2, 4):
        part = send(total.astype(bf16), to_z(flip))
        if flip == 4:
            part, done = lax.optimization_barrier((part, done))
        part = part.astype(f32)
        before = before + jnp.where((z ^ flip) < z, part, 0.0)
        total, before = lax.optimization_barrier((total + part, before))
        if flip == 1:
            total, halo = lax.optimization_barrier((total, halo))
        if flip == 2:
            total, halo = lax.optimization_barrier((total, halo))
            done = beside(halo)
    short = total.astype(bf16)
    for steps in (1, 2, 3):
        before = before + send(short, to_y(steps)).astype(f32)
    theirs = send((before + add[0]).astype(bf16), to_core)
    ours = before + add[1]
    return ours, theirs, done


def shape(dims, kind):
    return jax.ShapeDtypeStruct(dims, kind)


def project(parts, wf, ww, tables):
    tok_rows = parts[0].shape[0]
    wide = 2 * ww.shape[2] // 3
    queries = shape((tok_rows, wide + 2 * wf.shape[1]), bf16)
    tail = shape(((WMAX - 1) * BLOCK, 2 * wide), bf16)
    return pl.pallas_call(
        project_kernel,
        out_shape=(
            queries,
            shape((tok_rows, 2 * wide), bf16),
            tail,
            shape((ROWS, wide // 2), f32),
            shape((ROWS, wide // 2), bf16),
        ),
        in_specs=[HBM] * (N_TP + 1) + [VMEM] * 2,
        out_specs=(HBM, VMEM, HBM, VMEM, VMEM),
        scratch_shapes=[
            pltpu.VMEM((tok_rows, wf.shape[0]), bf16),
            pltpu.VMEM(wf.shape, bf16),
            pltpu.VMEM(queries.shape, bf16),
            pltpu.VMEM(tail.shape, bf16),
            pltpu.SemaphoreType.DMA((N_TP + 1,)),
        ],
        name="project",
        compiler_params=pltpu.CompilerParams(vmem_limit_bytes=LIMIT),
    )(*parts, wf, ww, tables.astype(bf16))


def near(win_blocks, qf, kv, halo, tables):
    tok_rows, wide = kv.shape[0], kv.shape[1] // 2
    return pl.pallas_call(
        local_kernel,
        out_shape=(
            shape((tok_rows, wide), f32),
            shape((tok_rows, wide), f32),
            shape((2, tok_rows, ROWS), bf16),
            shape((2, tok_rows, ROWS), bf16),
        ),
        in_specs=[SMEM, HBM, VMEM, VMEM, VMEM],
        out_specs=(VMEM,) * 4,
        scratch_shapes=[pltpu.VMEM(qf.shape, bf16), pltpu.SemaphoreType.DMA],
        name="near",
        compiler_params=pltpu.CompilerParams(vmem_limit_bytes=LIMIT),
    )(win_blocks, qf, kv, halo, tables.astype(bf16))


def hidden_rows(ours, theirs, near_out, win_out, high, low):
    tok_rows, wide = near_out.shape
    return pl.pallas_call(
        hidden_kernel,
        out_shape=(shape((tok_rows // 2, wide), bf16),) * 2,
        in_specs=[VMEM] * 6,
        out_specs=(VMEM,) * 2,
        scratch_shapes=[pltpu.VMEM((N_TP, tok_rows // N_TP, wide), bf16)],
        name="hidden",
        compiler_params=pltpu.CompilerParams(vmem_limit_bytes=LIMIT),
    )(ours, theirs, near_out, win_out, high, low)


def product(hidden, w_out):
    return pl.pallas_call(
        product_kernel,
        out_shape=(shape((hidden.shape[0] // NX, w_out.shape[1]), bf16),) * NX,
        in_specs=[VMEM] * 2,
        out_specs=(VMEM,) * NX,
        name="product",
        compiler_params=pltpu.CompilerParams(vmem_limit_bytes=LIMIT),
    )(hidden, w_out)


LIMIT = 12 * 2**20


def local(tokens, w_feature, w_window, w_out, win_blocks):
    model_width, head_count = w_feature.shape[:2]
    feat_dim = w_feature.shape[2] // 2
    seq, tp = lax.axis_index("seq"), lax.axis_index("tp")
    x, h, y, z, c = tp // 2, tp % 2, seq // (2 * NZ), seq // 2 % NZ, seq % 2

    other = send(tokens, to_half)
    parts = [tokens] + [send(tokens, to_x(s)) for s in (1, 3, 2)]
    w_out = w_out.reshape(-1, model_width)
    parts += [other] + [send(other, to_x(s)) for s in (1, 3, 2)]
    tables = feature_maps(feat_dim, head_count)
    qf, kv, tail, mine, theirs = project(
        parts, w_feature.reshape(model_width, -1), w_window.transpose(1, 0, 2), tables
    )

    def beside(halo):
        return near(win_blocks, qf, kv, halo, tables)

    ours, theirs, attended = prefix(mine, theirs, (x, h, y, z, c), send(tail, to_next), beside)
    keep, away = hidden_rows(ours, theirs, *attended)

    def summed(total, group):
        for steps in (1, 3, 2):
            total = total + send(group[steps], to_x(steps)).astype(f32)
        return total.astype(bf16)

    group = product(away, w_out)
    away, keep = lax.optimization_barrier((summed(group[0].astype(f32), group), keep))
    group = product(keep, w_out)
    total = lax.optimization_barrier(group[0].astype(f32) + send(away, to_half).astype(f32))
    return summed(total, group)


def solution(mesh):
    in_specs = (P("seq", "tp"), P(None, "tp", None), P(None, "tp", None), P("tp", None, None), P("tp"))
    return jax.shard_map(local, mesh=mesh, in_specs=in_specs, out_specs=P(("seq", "tp"), None), check_vma=False)
```

```python
import jax
import jax.numpy as jnp
import numpy as np
from jax import lax
from jax.experimental import pallas as pl
from jax.experimental.pallas import tpu as pltpu
from jax.sharding import PartitionSpec as P

BLOCK = 128
WMAX = 4
NX, NY, NZ = 4, 4, 8
N_TP = 8
EPS = 1e-06
SCALE = 12.0
bf16, f32 = jnp.bfloat16, jnp.float32


def pairs(move):
    out = []
    for x in range(NX):
        for h in range(2):
            for y in range(NY):
                for z in range(NZ):
                    for c in range(2):
                        to = move(x, h, y, z, c)
                        if to is not None:
                            tx, th, ty, tz, tc = to
                            source = ((y * NZ + z) * 2 + c) * N_TP + x * 2 + h
                            target = ((ty * NZ + tz) * 2 + tc) * N_TP + (tx % NX) * 2 + th
                            out.append((source, target))
    return out


def send(value, move):
    return lax.ppermute(value, ("seq", "tp"), pairs(move))


def to_x(steps):
    return lambda x, h, y, z, c: (x + steps, h, y, z, c)


def to_half(x, h, y, z, c):
    return (x, 1 - h, y, z, c)


def to_core(x, h, y, z, c):
    return (x, h, y, z, 1 - c)


def to_z(flip):
    return lambda x, h, y, z, c: (x, h, y, z ^ flip, c)


def to_y(steps):
    return lambda x, h, y, z, c: (x, h, y + steps, z, c) if y + steps < NY else None


def to_next(x, h, y, z, c):
    place = (y * NZ + z) * 2 + c + 1
    if place == NY * NZ * 2:
        return None
    return (x, h, place // (2 * NZ), place // 2 % NZ, place % 2)


ROWS = 160
EARLY = 256
PARTS = 2 * NX
VMEM = pl.BlockSpec(memory_space=pltpu.VMEM)
HBM = pl.BlockSpec(memory_space=pltpu.HBM)
SMEM = pl.BlockSpec(memory_space=pltpu.SMEM)


def feature_maps(feat_dim, heads):
    width = heads * 2 * feat_dim
    tables = np.zeros((heads, 4, ROWS, 2 * width), np.float32)
    at = 0
    for i in range(feat_dim):
        for j in range(i, feat_dim):
            for head in range(heads):
                query, key = head * 2 * feat_dim, (head * 2 + 1) * feat_dim
                tables[head, 0, at, query + i] = 1.0 / 32.0 if i == j else 1.0 / 16.0
                tables[head, 1, at, query + j] = 1.0
                tables[head, 2, at, key + i] = 1.0
                tables[head, 3, at, key + j] = 1.0
            at += 1
    for i in range(feat_dim):
        for head in range(heads):
            query, key = head * 2 * feat_dim, (head * 2 + 1) * feat_dim
            tables[head, 0, at, query + i] = 0.25
            tables[head, 2, at, key + i] = 1.0
        tables[:, 1::2, at, width] = 1.0
        at += 1
    tables[:, :, at, width] = 1.0
    return tables


def dot(a, b):
    return jnp.dot(a, b, preferred_element_type=f32)


def dot_t(a, b):
    return lax.dot_general(a, b, (((1,), (1,)), ((), ())), preferred_element_type=f32)


def unit(v):
    return v * lax.rsqrt(jnp.mean(v * v, axis=-1, keepdims=True) + EPS)


def halves(v):
    high = v.astype(bf16)
    return high, (v - high.astype(f32)).astype(bf16)


def position():
    seq, tp = lax.axis_index("seq"), lax.axis_index("tp")
    return lax.div(tp, 2), lax.rem(tp, 2), lax.rem(seq, 2), seq


def project_kernel(*refs):
    parts = refs[:PARTS]
    wf, ww, table, qf_ref, kv_ref, tail_ref, mine_ref, other_ref, held, held_wf, qf, tail, sems = refs[PARTS:]
    x, half, core, _ = position()
    width = parts[0].shape[1]
    head = ww.shape[2] // 3
    rows = held.shape[0]
    copies = []
    for k, s in enumerate((0, 1, 3, 2)):
        column = lax.rem(x + NX - s, NX) * 2
        for part, first, count, side, to in (
            (parts[k], 0, rows, half, 0),
            (parts[k], rows, EARLY, 1 - half, 0),
            (parts[NX + k], 0, rows - EARLY, 1 - half, EARLY),
        ):
            cols = pl.ds(pl.multiple_of((column + side) * width, width), width)
            target = held.at[pl.ds(to, count), cols]
            copies.append(pltpu.make_async_copy(part.at[pl.ds(first, count)], target, sems.at[len(copies)]))
    copies.append(pltpu.make_async_copy(wf, held_wf, sems.at[len(copies)]))
    for copy in copies:
        copy.start()
    for copy in copies:
        copy.wait()
    tokens = held[...]

    def columns(weight):
        return dot(tokens, weight).astype(bf16)

    feats = columns(held_wf[...])
    ones = lax.broadcasted_iota(jnp.int32, feats.shape, 1) == 0
    feats = jnp.concatenate([feats, jnp.where(ones, 1.0, 0.0).astype(bf16)], axis=1)
    qf[:, 2 * head :] = feats
    first_tail = kv_ref.shape[0] - tail.shape[0]
    leave = [pltpu.make_async_copy(tail, tail_ref, sems.at[0]), pltpu.make_async_copy(qf, qf_ref, sems.at[1])]
    for kind in (2, 1, 0):
        out = columns(jnp.concatenate([ww[h, :, kind * head : (kind + 1) * head] for h in range(2)], axis=1))
        if kind == 2:
            values = out
            kv_ref[:, 2 * head :] = out
            tail[:, 2 * head :] = out[first_tail:]
            continue
        for h in range(2):
            cols = slice(h * head, (h + 1) * head)
            normed = unit(out[:, cols].astype(f32)).astype(bf16)
            if kind == 1:
                kv_ref[:, cols] = normed
                tail[:, cols] = normed[first_tail:]
            else:
                qf[:, cols] = normed
        leave[1 - kind].start()
    states = []
    for h in range(2):
        left = dot_t(table[h, 2], feats)
        right = dot_t(table[h, 3], feats)
        high, low = halves(left * right)
        v = values[:, h * head : (h + 1) * head]
        states.append(dot(high, v) + dot(low, v))
    mine_ref[...] = jnp.where(core == 0, states[0], states[1])
    other_ref[...] = jnp.where(core == 0, states[1], states[0]).astype(bf16)
    for copy in leave:
        copy.wait()


def local_kernel(win, qf_ref, kv_ref, halo_ref, table, near_ref, win_ref, high_ref, low_ref, qn_ref, sem):
    copy = pltpu.make_async_copy(qf_ref, qn_ref, sem)
    copy.start()
    copy.wait()
    seq = position()[3]
    rows = qn_ref.shape[0]
    heads = win_ref.shape[1] // 128
    head = 128
    halo = halo_ref.shape[0]
    span = halo + BLOCK
    feats = qn_ref[:, heads * head :]
    feat = feats.shape[1] // (4 * heads)
    blocks = rows // BLOCK
    row = lax.broadcasted_iota(jnp.int32, (BLOCK, span), 0)
    col = lax.broadcasted_iota(jnp.int32, (BLOCK, span), 1)
    causal = col <= row + halo
    for h in range(heads):
        cols = slice(h * head, (h + 1) * head)
        vcols = slice((heads + h) * head, (heads + h + 1) * head)
        left = dot_t(feats, table[h, 0])
        right = dot_t(feats, table[h, 1])
        high, low = halves(left * right)
        high_ref[h] = high
        low_ref[h] = low
        key = lax.broadcasted_iota(jnp.int32, (feats.shape[1], feats.shape[1]), 0)
        lane = lax.broadcasted_iota(jnp.int32, (feats.shape[1], feats.shape[1]), 1)
        first = h * 2 * feat
        moved = (lane == key + feat) & (key >= first) & (key < first + feat)
        query = dot(feats, jnp.where(moved, 1.0, 0.0).astype(bf16)).astype(bf16)
        keys = jnp.concatenate([halo_ref[:, cols], kv_ref[:, cols]], axis=0)
        values = jnp.concatenate([halo_ref[:, vcols], kv_ref[:, vcols]], axis=0)
        for b in range(blocks):
            at = slice(b * BLOCK, (b + 1) * BLOCK)
            ahead = (b + 1) * BLOCK
            inner = dot_t(query[at], feats[:ahead])
            pair = 1.0 + inner * (0.25 + inner * (1.0 / 32.0))
            last = jnp.where(causal[:, halo:], pair[:, b * BLOCK :], 0.0)
            pair = jnp.concatenate([pair[:, : b * BLOCK], last], axis=1) if b else last
            near_ref[at, cols] = dot(pair.astype(bf16), values[halo : halo + ahead])
            scores = dot_t(qn_ref[at, cols], keys[b * BLOCK : b * BLOCK + span]) * (SCALE / head)
            least = jnp.maximum(span // BLOCK - win[h], span // BLOCK - 1 - (seq * blocks + b))
            allowed = causal & (col >= least * BLOCK)
            weights = jnp.where(allowed, jnp.exp(scores), 0.0).astype(bf16)
            win_ref[at, cols] = unit(dot(weights, values[b * BLOCK : b * BLOCK + span]))


def hidden_kernel(ours, theirs, near_ref, win_ref, high_ref, low_ref, keep_ref, away_ref, hidden):
    x, half, core, _ = position()
    mine, other = ours[...], theirs[...].astype(f32)
    head = mine.shape[1]
    rows = hidden.shape[1]
    for h in range(2):
        cols = slice(h * head, (h + 1) * head)
        state_high, state_low = halves(jnp.where(core == h, mine, other))
        high = high_ref[h]
        far = dot(high, state_high) + dot(low_ref[h], state_high) + dot(high, state_low)
        out = (unit(near_ref[:, cols] + far) + win_ref[:, cols]).astype(bf16)
        for g in range(N_TP):
            hidden[g, :, cols] = out[g * rows : (g + 1) * rows]
    for s in range(NX):
        group = lax.rem(x + s, NX) * 2
        keep_ref[s * rows : (s + 1) * rows] = hidden[group + half]
        away_ref[s * rows : (s + 1) * rows] = hidden[group + 1 - half]


def product_kernel(hidden_ref, w_ref, *outs):
    rows = outs[0].shape[0]
    product = dot(hidden_ref[...], w_ref[...]).astype(bf16)
    for s, out in enumerate(outs):
        out[...] = product[s * rows : (s + 1) * rows]


def prefix(mine, other, place, halo, beside):
    x, h, y, z, c = place
    got = send(other, to_core).astype(f32)
    total = mine + got
    add = (jnp.where(c == 0, mine, 0.0), jnp.where(c == 1, got, 0.0))
    total, add = lax.optimization_barrier((total, add))
    before = jnp.zeros_like(total)
    done = None
    for flip in (1, 2, 4):
        part = send(total.astype(bf16), to_z(flip))
        if flip == 4:
            part, done = lax.optimization_barrier((part, done))
        part = part.astype(f32)
        before = before + jnp.where((z ^ flip) < z, part, 0.0)
        total, before = lax.optimization_barrier((total + part, before))
        if flip == 1:
            total, halo = lax.optimization_barrier((total, halo))
        if flip == 2:
            total, halo = lax.optimization_barrier((total, halo))
            done = beside(halo)
    short = total.astype(bf16)
    for steps in (1, 2, 3):
        before = before + send(short, to_y(steps)).astype(f32)
    theirs = send((before + add[0]).astype(bf16), to_core)
    ours = before + add[1]
    return ours, theirs, done


def shape(dims, kind):
    return jax.ShapeDtypeStruct(dims, kind)


def project(parts, wf, ww, tables):
    tok_rows = parts[0].shape[0] - EARLY
    wide = 2 * ww.shape[2] // 3
    queries = shape((tok_rows, wide + 2 * wf.shape[1]), bf16)
    tail = shape(((WMAX - 1) * BLOCK, 2 * wide), bf16)
    return pl.pallas_call(
        project_kernel,
        out_shape=(
            queries,
            shape((tok_rows, 2 * wide), bf16),
            tail,
            shape((ROWS, wide // 2), f32),
            shape((ROWS, wide // 2), bf16),
        ),
        in_specs=[HBM] * (PARTS + 1) + [VMEM] * 2,
        out_specs=(HBM, VMEM, HBM, VMEM, VMEM),
        scratch_shapes=[
            pltpu.VMEM((tok_rows, wf.shape[0]), bf16),
            pltpu.VMEM(wf.shape, bf16),
            pltpu.VMEM(queries.shape, bf16),
            pltpu.VMEM(tail.shape, bf16),
            pltpu.SemaphoreType.DMA((3 * NX + 1,)),
        ],
        name="project",
        compiler_params=pltpu.CompilerParams(vmem_limit_bytes=LIMIT),
    )(*parts, wf, ww, tables.astype(bf16))


def near(win_blocks, qf, kv, halo, tables):
    tok_rows, wide = kv.shape[0], kv.shape[1] // 2
    return pl.pallas_call(
        local_kernel,
        out_shape=(
            shape((tok_rows, wide), f32),
            shape((tok_rows, wide), f32),
            shape((2, tok_rows, ROWS), bf16),
            shape((2, tok_rows, ROWS), bf16),
        ),
        in_specs=[SMEM, HBM, VMEM, VMEM, VMEM],
        out_specs=(VMEM,) * 4,
        scratch_shapes=[pltpu.VMEM(qf.shape, bf16), pltpu.SemaphoreType.DMA],
        name="near",
        compiler_params=pltpu.CompilerParams(vmem_limit_bytes=LIMIT),
    )(win_blocks, qf, kv, halo, tables.astype(bf16))


def hidden_rows(ours, theirs, near_out, win_out, high, low):
    tok_rows, wide = near_out.shape
    return pl.pallas_call(
        hidden_kernel,
        out_shape=(shape((tok_rows // 2, wide), bf16),) * 2,
        in_specs=[VMEM] * 6,
        out_specs=(VMEM,) * 2,
        scratch_shapes=[pltpu.VMEM((N_TP, tok_rows // N_TP, wide), bf16)],
        name="hidden",
        compiler_params=pltpu.CompilerParams(vmem_limit_bytes=LIMIT),
    )(ours, theirs, near_out, win_out, high, low)


def product(hidden, w_out):
    return pl.pallas_call(
        product_kernel,
        out_shape=(shape((hidden.shape[0] // NX, w_out.shape[1]), bf16),) * NX,
        in_specs=[VMEM] * 2,
        out_specs=(VMEM,) * NX,
        name="product",
        compiler_params=pltpu.CompilerParams(vmem_limit_bytes=LIMIT),
    )(hidden, w_out)


LIMIT = 12 * 2**20


def local(tokens, w_feature, w_window, w_out, win_blocks):
    model_width, head_count = w_feature.shape[:2]
    feat_dim = w_feature.shape[2] // 2
    seq, tp = lax.axis_index("seq"), lax.axis_index("tp")
    x, h, y, z, c = tp // 2, tp % 2, seq // (2 * NZ), seq // 2 % NZ, seq % 2

    first, second = [send(piece, to_half) for piece in jnp.split(tokens, [EARLY])]
    first = jnp.concatenate([tokens, first], axis=0)
    wf, ww = w_feature.reshape(model_width, -1), w_window.transpose(1, 0, 2)
    parts = [part for source in (first, second) for part in [source] + [send(source, to_x(s)) for s in (1, 3, 2)]]
    w_out = w_out.reshape(-1, model_width)
    tables = feature_maps(feat_dim, head_count)
    qf, kv, tail, mine, theirs = project(
        parts, wf, ww, tables
    )

    def beside(halo):
        return near(win_blocks, qf, kv, halo, tables)

    ours, theirs, attended = prefix(mine, theirs, (x, h, y, z, c), send(tail, to_next), beside)
    keep, away = hidden_rows(ours, theirs, *attended)

    def summed(total, group):
        for steps in (1, 3, 2):
            total = total + send(group[steps], to_x(steps)).astype(f32)
        return total.astype(bf16)

    group = product(away, w_out)
    away, keep = lax.optimization_barrier((summed(group[0].astype(f32), group), keep))
    group = product(keep, w_out)
    total = lax.optimization_barrier(group[0].astype(f32) + send(away, to_half).astype(f32))
    return summed(total, group)


def solution(mesh):
    in_specs = (P("seq", "tp"), P(None, "tp", None), P(None, "tp", None), P("tp", None, None), P("tp"))
    return jax.shard_map(local, mesh=mesh, in_specs=in_specs, out_specs=P(("seq", "tp"), None), check_vma=False)
```

```python
import jax
import jax.numpy as jnp
import numpy as np
from jax import lax
from jax.experimental import pallas as pl
from jax.experimental.pallas import tpu as pltpu
from jax.sharding import PartitionSpec as P

BLOCK = 128
WMAX = 4
NX, NY, NZ = 4, 4, 8
N_TP = 8
EPS = 1e-06
SCALE = 12.0
bf16, f32 = jnp.bfloat16, jnp.float32


def pairs(move):
    out = []
    for x in range(NX):
        for h in range(2):
            for y in range(NY):
                for z in range(NZ):
                    for c in range(2):
                        to = move(x, h, y, z, c)
                        if to is not None:
                            tx, th, ty, tz, tc = to
                            source = ((y * NZ + z) * 2 + c) * N_TP + x * 2 + h
                            target = ((ty * NZ + tz) * 2 + tc) * N_TP + (tx % NX) * 2 + th
                            out.append((source, target))
    return out


def send(value, move):
    return lax.ppermute(value, ("seq", "tp"), pairs(move))


def to_x(steps):
    return lambda x, h, y, z, c: (x + steps, h, y, z, c)


def to_half(x, h, y, z, c):
    return (x, 1 - h, y, z, c)


def to_core(x, h, y, z, c):
    return (x, h, y, z, 1 - c)


def to_z(flip):
    return lambda x, h, y, z, c: (x, h, y, z ^ flip, c)


def to_y(steps):
    return lambda x, h, y, z, c: (x, h, y + steps, z, c) if y + steps < NY else None


def to_next(x, h, y, z, c):
    place = (y * NZ + z) * 2 + c + 1
    if place == NY * NZ * 2:
        return None
    return (x, h, place // (2 * NZ), place // 2 % NZ, place % 2)


ROWS = 160
VMEM = pl.BlockSpec(memory_space=pltpu.VMEM)
HBM = pl.BlockSpec(memory_space=pltpu.HBM)
SMEM = pl.BlockSpec(memory_space=pltpu.SMEM)


def feature_maps(feat_dim, heads):
    width = heads * 2 * feat_dim
    tables = np.zeros((heads, 4, ROWS, 2 * width), np.float32)
    at = 0
    for i in range(feat_dim):
        for j in range(i, feat_dim):
            for head in range(heads):
                query, key = head * 2 * feat_dim, (head * 2 + 1) * feat_dim
                tables[head, 0, at, query + i] = 1.0 / 32.0 if i == j else 1.0 / 16.0
                tables[head, 1, at, query + j] = 1.0
                tables[head, 2, at, key + i] = 1.0
                tables[head, 3, at, key + j] = 1.0
            at += 1
    for i in range(feat_dim):
        for head in range(heads):
            query, key = head * 2 * feat_dim, (head * 2 + 1) * feat_dim
            tables[head, 0, at, query + i] = 0.25
            tables[head, 2, at, key + i] = 1.0
        tables[:, 1::2, at, width] = 1.0
        at += 1
    tables[:, :, at, width] = 1.0
    return tables


def dot(a, b):
    return jnp.dot(a, b, preferred_element_type=f32)


def dot_t(a, b):
    return lax.dot_general(a, b, (((1,), (1,)), ((), ())), preferred_element_type=f32)


def unit(v):
    return v * lax.rsqrt(jnp.mean(v * v, axis=-1, keepdims=True) + EPS)


def halves(v):
    high = v.astype(bf16)
    return high, (v - high.astype(f32)).astype(bf16)


def position():
    seq, tp = lax.axis_index("seq"), lax.axis_index("tp")
    return lax.div(tp, 2), lax.rem(tp, 2), lax.rem(seq, 2), seq


def project_kernel(*refs):
    parts = refs[:N_TP]
    wf, ww, table, qf_ref, kv_ref, tail_ref, mine_ref, short_ref, other_ref, held, held_wf, qf, tail, sems = refs[N_TP:]
    x, half, core, _ = position()
    owners = [lax.rem(x + NX - s, NX) * 2 + side for side in (half, 1 - half) for s in (0, 1, 3, 2)]
    width = parts[0].shape[1]
    head = ww.shape[2] // 3
    copies = [
        pltpu.make_async_copy(part, held.at[:, pl.ds(pl.multiple_of(owner * width, width), width)], sems.at[k])
        for k, (part, owner) in enumerate(zip(parts, owners))
    ]
    copies.append(pltpu.make_async_copy(wf, held_wf, sems.at[N_TP]))
    for copy in copies:
        copy.start()
    for copy in copies:
        copy.wait()
    tokens = held[...]

    def columns(weight):
        return dot(tokens, weight).astype(bf16)

    feats = dot_t(tokens, held_wf[...]).astype(bf16)
    ones = lax.broadcasted_iota(jnp.int32, feats.shape, 1) == 0
    feats = jnp.concatenate([feats, jnp.where(ones, 1.0, 0.0).astype(bf16)], axis=1)
    qf[:, 2 * head :] = feats
    first_tail = kv_ref.shape[0] - tail.shape[0]
    leave = [pltpu.make_async_copy(tail, tail_ref, sems.at[0]), pltpu.make_async_copy(qf, qf_ref, sems.at[1])]
    for kind in (2, 1, 0):
        out = columns(jnp.concatenate([ww[h, :, kind * head : (kind + 1) * head] for h in range(2)], axis=1))
        if kind == 2:
            values = out
            kv_ref[:, 2 * head :] = out
            tail[:, 2 * head :] = out[first_tail:]
            continue
        for h in range(2):
            cols = slice(h * head, (h + 1) * head)
            normed = unit(out[:, cols].astype(f32)).astype(bf16)
            if kind == 1:
                kv_ref[:, cols] = normed
                tail[:, cols] = normed[first_tail:]
            else:
                qf[:, cols] = normed
        leave[1 - kind].start()
    states = []
    for h in range(2):
        left = dot_t(table[h, 2], feats)
        right = dot_t(table[h, 3], feats)
        high, low = halves(left * right)
        v = values[:, h * head : (h + 1) * head]
        states.append(dot(high, v) + dot(low, v))
    mine = jnp.where(core == 0, states[0], states[1])
    mine_ref[...] = mine
    short_ref[...] = mine.astype(bf16)
    other_ref[...] = jnp.where(core == 0, states[1], states[0]).astype(bf16)
    for copy in leave:
        copy.wait()


def local_kernel(win, qf_ref, kv_ref, halo_ref, table, near_ref, win_ref, high_ref, low_ref, qn_ref, sem):
    copy = pltpu.make_async_copy(qf_ref, qn_ref, sem)
    copy.start()
    copy.wait()
    seq = position()[3]
    rows = qn_ref.shape[0]
    heads = win_ref.shape[1] // 128
    head = 128
    halo = halo_ref.shape[0]
    span = halo + BLOCK
    feats = qn_ref[:, heads * head :]
    feat = feats.shape[1] // (4 * heads)
    blocks = rows // BLOCK
    row = lax.broadcasted_iota(jnp.int32, (BLOCK, span), 0)
    col = lax.broadcasted_iota(jnp.int32, (BLOCK, span), 1)
    causal = col <= row + halo
    for h in range(heads):
        cols = slice(h * head, (h + 1) * head)
        vcols = slice((heads + h) * head, (heads + h + 1) * head)
        left = dot_t(feats, table[h, 0])
        right = dot_t(feats, table[h, 1])
        high, low = halves(left * right)
        high_ref[h] = high
        low_ref[h] = low
        key = lax.broadcasted_iota(jnp.int32, (feats.shape[1], feats.shape[1]), 0)
        lane = lax.broadcasted_iota(jnp.int32, (feats.shape[1], feats.shape[1]), 1)
        first = h * 2 * feat
        moved = (lane == key + feat) & (key >= first) & (key < first + feat)
        query = dot(feats, jnp.where(moved, 1.0, 0.0).astype(bf16)).astype(bf16)
        keys = jnp.concatenate([halo_ref[:, cols], kv_ref[:, cols]], axis=0)
        values = jnp.concatenate([halo_ref[:, vcols], kv_ref[:, vcols]], axis=0)
        for b in range(blocks):
            at = slice(b * BLOCK, (b + 1) * BLOCK)
            ahead = (b + 1) * BLOCK
            inner = dot_t(query[at], feats[:ahead])
            pair = 1.0 + inner * (0.25 + inner * (1.0 / 32.0))
            last = jnp.where(causal[:, halo:], pair[:, b * BLOCK :], 0.0)
            pair = jnp.concatenate([pair[:, : b * BLOCK], last], axis=1) if b else last
            near_ref[at, cols] = dot(pair.astype(bf16), values[halo : halo + ahead])
            scores = dot_t(qn_ref[at, cols], keys[b * BLOCK : b * BLOCK + span]) * (SCALE / head)
            least = jnp.maximum(span // BLOCK - win[h], span // BLOCK - 1 - (seq * blocks + b))
            allowed = causal & (col >= least * BLOCK)
            weights = jnp.where(allowed, jnp.exp(scores), 0.0).astype(bf16)
            win_ref[at, cols] = unit(dot(weights, values[b * BLOCK : b * BLOCK + span]))


def hidden_kernel(ours, theirs, near_ref, win_ref, high_ref, low_ref, keep_ref, away_ref, hidden):
    x, half, core, _ = position()
    mine, other = ours[...], theirs[...].astype(f32)
    head = mine.shape[1]
    rows = hidden.shape[1]
    for h in range(2):
        cols = slice(h * head, (h + 1) * head)
        state_high, state_low = halves(jnp.where(core == h, mine, other))
        high = high_ref[h]
        far = dot(high, state_high) + dot(low_ref[h], state_high) + dot(high, state_low)
        out = (unit(near_ref[:, cols] + far) + win_ref[:, cols]).astype(bf16)
        for g in range(N_TP):
            hidden[g, :, cols] = out[g * rows : (g + 1) * rows]
    for s in range(NX):
        group = lax.rem(x + s, NX) * 2
        keep_ref[s * rows : (s + 1) * rows] = hidden[group + half]
        away_ref[s * rows : (s + 1) * rows] = hidden[group + 1 - half]


def product_kernel(hidden_ref, w_ref, *outs):
    rows = outs[0].shape[0]
    product = dot(hidden_ref[...], w_ref[...]).astype(bf16)
    for s, out in enumerate(outs):
        out[...] = product[s * rows : (s + 1) * rows]


def prefix(mine, short, other, place, halo, beside):
    x, h, y, z, c = place
    across = send(other, lambda x, h, y, z, c: (x, h, y, z ^ 1, 1 - c)).astype(f32)
    beyond = send(short, to_z(1)).astype(f32)
    got = send(other, to_core).astype(f32)
    total = mine + got + across + beyond
    add = (jnp.where(c == 0, mine, 0.0), jnp.where(c == 1, got, 0.0))
    before = jnp.where(z % 2 == 1, across + beyond, 0.0)
    total, before, add = lax.optimization_barrier((total, before, add))
    done = None
    for flip in (2, 4):
        part = send(total.astype(bf16), to_z(flip))
        if flip == 4:
            part, done = lax.optimization_barrier((part, done))
        part = part.astype(f32)
        before = before + jnp.where((z ^ flip) < z, part, 0.0)
        total, before = lax.optimization_barrier((total + part, before))
        if flip == 2:
            total, halo = lax.optimization_barrier((total, halo))
            done = beside(halo)
    short = total.astype(bf16)
    for steps in (1, 2, 3):
        before = before + send(short, to_y(steps)).astype(f32)
    theirs = send((before + add[0]).astype(bf16), to_core)
    ours = before + add[1]
    return ours, theirs, done


def shape(dims, kind):
    return jax.ShapeDtypeStruct(dims, kind)


def project(parts, wf, ww, tables):
    tok_rows = parts[0].shape[0]
    wide = 2 * ww.shape[2] // 3
    queries = shape((tok_rows, wide + 2 * wf.shape[0]), bf16)
    tail = shape(((WMAX - 1) * BLOCK, 2 * wide), bf16)
    return pl.pallas_call(
        project_kernel,
        out_shape=(
            queries,
            shape((tok_rows, 2 * wide), bf16),
            tail,
            shape((ROWS, wide // 2), f32),
            shape((ROWS, wide // 2), bf16),
            shape((ROWS, wide // 2), bf16),
        ),
        in_specs=[HBM] * (N_TP + 1) + [VMEM] * 2,
        out_specs=(HBM, VMEM, HBM, VMEM, VMEM, VMEM),
        scratch_shapes=[
            pltpu.VMEM((tok_rows, wf.shape[1]), bf16),
            pltpu.VMEM(wf.shape, bf16),
            pltpu.VMEM(queries.shape, bf16),
            pltpu.VMEM(tail.shape, bf16),
            pltpu.SemaphoreType.DMA((N_TP + 1,)),
        ],
        name="project",
        compiler_params=pltpu.CompilerParams(vmem_limit_bytes=LIMIT),
    )(*parts, wf, ww, tables.astype(bf16))


def near(win_blocks, qf, kv, halo, tables):
    tok_rows, wide = kv.shape[0], kv.shape[1] // 2
    return pl.pallas_call(
        local_kernel,
        out_shape=(
            shape((tok_rows, wide), f32),
            shape((tok_rows, wide), f32),
            shape((2, tok_rows, ROWS), bf16),
            shape((2, tok_rows, ROWS), bf16),
        ),
        in_specs=[SMEM, HBM, VMEM, VMEM, VMEM],
        out_specs=(VMEM,) * 4,
        scratch_shapes=[pltpu.VMEM(qf.shape, bf16), pltpu.SemaphoreType.DMA],
        name="near",
        compiler_params=pltpu.CompilerParams(vmem_limit_bytes=LIMIT),
    )(win_blocks, qf, kv, halo, tables.astype(bf16))


def hidden_rows(ours, theirs, near_out, win_out, high, low):
    tok_rows, wide = near_out.shape
    return pl.pallas_call(
        hidden_kernel,
        out_shape=(shape((tok_rows // 2, wide), bf16),) * 2,
        in_specs=[VMEM] * 6,
        out_specs=(VMEM,) * 2,
        scratch_shapes=[pltpu.VMEM((N_TP, tok_rows // N_TP, wide), bf16)],
        name="hidden",
        compiler_params=pltpu.CompilerParams(vmem_limit_bytes=LIMIT),
    )(ours, theirs, near_out, win_out, high, low)


def product(hidden, w_out):
    return pl.pallas_call(
        product_kernel,
        out_shape=(shape((hidden.shape[0] // NX, w_out.shape[1]), bf16),) * NX,
        in_specs=[VMEM] * 2,
        out_specs=(VMEM,) * NX,
        name="product",
        compiler_params=pltpu.CompilerParams(vmem_limit_bytes=LIMIT),
    )(hidden, w_out)


LIMIT = 12 * 2**20


def local(tokens, w_feature, w_window, w_out, win_blocks):
    model_width, head_count = w_feature.shape[:2]
    feat_dim = w_feature.shape[2] // 2
    seq, tp = lax.axis_index("seq"), lax.axis_index("tp")
    x, h, y, z, c = tp // 2, tp % 2, seq // (2 * NZ), seq // 2 % NZ, seq % 2

    other = send(tokens, to_half)
    parts = [tokens] + [send(tokens, to_x(s)) for s in (1, 3, 2)]
    w_out = w_out.reshape(-1, model_width)
    parts += [other] + [send(other, to_x(s)) for s in (1, 3, 2)]
    tables = feature_maps(feat_dim, head_count)
    qf, kv, tail, mine, short, theirs = project(
        parts, w_feature.transpose(1, 2, 0).reshape(-1, model_width), w_window.transpose(1, 0, 2), tables
    )

    def beside(halo):
        return near(win_blocks, qf, kv, halo, tables)

    ours, theirs, attended = prefix(mine, short, theirs, (x, h, y, z, c), send(tail, to_next), beside)
    keep, away = hidden_rows(ours, theirs, *attended)

    def summed(total, group):
        for steps in (1, 3, 2):
            total = total + send(group[steps], to_x(steps)).astype(f32)
        return total.astype(bf16)

    group = product(away, w_out)
    away, keep = lax.optimization_barrier((summed(group[0].astype(f32), group), keep))
    group = product(keep, w_out)
    total = lax.optimization_barrier(group[0].astype(f32) + send(away, to_half).astype(f32))
    return summed(total, group)


def solution(mesh):
    in_specs = (P("seq", "tp"), P(None, "tp", None), P(None, "tp", None), P("tp", None, None), P("tp"))
    return jax.shard_map(local, mesh=mesh, in_specs=in_specs, out_specs=P(("seq", "tp"), None), check_vma=False)
```

```python
import jax
import jax.numpy as jnp
import numpy as np
from jax import lax
from jax.experimental import pallas as pl
from jax.experimental.pallas import tpu as pltpu
from jax.sharding import PartitionSpec as P

BLOCK = 128
WMAX = 4
NX, NY, NZ = 4, 4, 8
N_TP = 8
EPS = 1e-06
SCALE = 12.0
bf16, f32 = jnp.bfloat16, jnp.float32


def pairs(move):
    out = []
    for x in range(NX):
        for h in range(2):
            for y in range(NY):
                for z in range(NZ):
                    for c in range(2):
                        to = move(x, h, y, z, c)
                        if to is not None:
                            tx, th, ty, tz, tc = to
                            source = ((y * NZ + z) * 2 + c) * N_TP + x * 2 + h
                            target = ((ty * NZ + tz) * 2 + tc) * N_TP + (tx % NX) * 2 + th
                            out.append((source, target))
    return out


def send(value, move):
    return lax.ppermute(value, ("seq", "tp"), pairs(move))


def to_x(steps):
    return lambda x, h, y, z, c: (x + steps, h, y, z, c)


def to_half(x, h, y, z, c):
    return (x, 1 - h, y, z, c)


def to_core(x, h, y, z, c):
    return (x, h, y, z, 1 - c)


def to_z(flip):
    return lambda x, h, y, z, c: (x, h, y, z ^ flip, c)


def to_y(steps):
    return lambda x, h, y, z, c: (x, h, y + steps, z, c) if y + steps < NY else None


def to_next(x, h, y, z, c):
    place = (y * NZ + z) * 2 + c + 1
    if place == NY * NZ * 2:
        return None
    return (x, h, place // (2 * NZ), place // 2 % NZ, place % 2)


ROWS = 160
VMEM = pl.BlockSpec(memory_space=pltpu.VMEM)
HBM = pl.BlockSpec(memory_space=pltpu.HBM)
SMEM = pl.BlockSpec(memory_space=pltpu.SMEM)


def feature_maps(feat_dim, heads):
    width = heads * 2 * feat_dim
    tables = np.zeros((heads, 4, ROWS, 2 * width), np.float32)
    at = 0
    for i in range(feat_dim):
        for j in range(i, feat_dim):
            for head in range(heads):
                query, key = head * 2 * feat_dim, (head * 2 + 1) * feat_dim
                tables[head, 0, at, query + i] = 1.0 / 32.0 if i == j else 1.0 / 16.0
                tables[head, 1, at, query + j] = 1.0
                tables[head, 2, at, key + i] = 1.0
                tables[head, 3, at, key + j] = 1.0
            at += 1
    for i in range(feat_dim):
        for head in range(heads):
            query, key = head * 2 * feat_dim, (head * 2 + 1) * feat_dim
            tables[head, 0, at, query + i] = 0.25
            tables[head, 2, at, key + i] = 1.0
        tables[:, 1::2, at, width] = 1.0
        at += 1
    tables[:, :, at, width] = 1.0
    return tables


def dot(a, b):
    return jnp.dot(a, b, preferred_element_type=f32)


def dot_t(a, b):
    return lax.dot_general(a, b, (((1,), (1,)), ((), ())), preferred_element_type=f32)


def unit(v):
    return v * lax.rsqrt(jnp.mean(v * v, axis=-1, keepdims=True) + EPS)


def halves(v):
    high = v.astype(bf16)
    return high, (v - high.astype(f32)).astype(bf16)


def position():
    seq, tp = lax.axis_index("seq"), lax.axis_index("tp")
    return lax.div(tp, 2), lax.rem(tp, 2), lax.rem(seq, 2), seq


def project_kernel(*refs):
    parts = refs[:N_TP]
    wf, ww, table, qf_ref, kv_ref, tail_ref, mine_ref, short_ref, other_ref, held, held_wf, qf, tail, sems = refs[N_TP:]
    x, half, core, _ = position()
    owners = [lax.rem(x + NX - s, NX) * 2 + side for side in (half, 1 - half) for s in (0, 1, 3, 2)]
    width = parts[0].shape[1]
    head = ww.shape[2] // 3
    copies = [
        pltpu.make_async_copy(part, held.at[:, pl.ds(pl.multiple_of(owner * width, width), width)], sems.at[k])
        for k, (part, owner) in enumerate(zip(parts, owners))
    ]
    copies.append(pltpu.make_async_copy(wf, held_wf, sems.at[N_TP]))
    for copy in copies:
        copy.start()
    for copy in copies:
        copy.wait()
    tokens = held[...]

    def columns(weight):
        return dot(tokens, weight).astype(bf16)

    feats = dot_t(tokens, held_wf[...]).astype(bf16)
    ones = lax.broadcasted_iota(jnp.int32, feats.shape, 1) == 0
    feats = jnp.concatenate([feats, jnp.where(ones, 1.0, 0.0).astype(bf16)], axis=1)
    qf[:, 2 * head :] = feats
    first_tail = kv_ref.shape[0] - tail.shape[0]
    leave = [pltpu.make_async_copy(tail, tail_ref, sems.at[0]), pltpu.make_async_copy(qf, qf_ref, sems.at[1])]
    for kind in (2, 1, 0):
        out = columns(jnp.concatenate([ww[h, :, kind * head : (kind + 1) * head] for h in range(2)], axis=1))
        if kind == 2:
            values = out
            kv_ref[:, 2 * head :] = out
            tail[:, 2 * head :] = out[first_tail:]
            continue
        for h in range(2):
            cols = slice(h * head, (h + 1) * head)
            normed = unit(out[:, cols].astype(f32)).astype(bf16)
            if kind == 1:
                kv_ref[:, cols] = normed
                tail[:, cols] = normed[first_tail:]
            else:
                qf[:, cols] = normed
        leave[1 - kind].start()
    states = []
    for h in range(2):
        left = dot_t(table[h, 2], feats)
        right = dot_t(table[h, 3], feats)
        high, low = halves(left * right)
        v = values[:, h * head : (h + 1) * head]
        states.append(dot(high, v) + dot(low, v))
    mine = jnp.where(core == 0, states[0], states[1])
    mine_ref[...] = mine
    short_ref[...] = mine.astype(bf16)
    other_ref[...] = jnp.where(core == 0, states[1], states[0]).astype(bf16)
    for copy in leave:
        copy.wait()


def near_kernel(qf_ref, kv_ref, table, near_ref, high_ref, low_ref, qn_ref, sem):
    copy = pltpu.make_async_copy(qf_ref, qn_ref, sem)
    copy.start()
    copy.wait()
    rows = qn_ref.shape[0]
    heads = near_ref.shape[1] // 128
    head = 128
    feats = qn_ref[:, heads * head :]
    feat = feats.shape[1] // (4 * heads)
    row = lax.broadcasted_iota(jnp.int32, (BLOCK, BLOCK), 0)
    col = lax.broadcasted_iota(jnp.int32, (BLOCK, BLOCK), 1)
    for h in range(heads):
        cols = slice(h * head, (h + 1) * head)
        vcols = slice((heads + h) * head, (heads + h + 1) * head)
        left = dot_t(feats, table[h, 0])
        right = dot_t(feats, table[h, 1])
        high, low = halves(left * right)
        high_ref[h] = high
        low_ref[h] = low
        key = lax.broadcasted_iota(jnp.int32, (feats.shape[1], feats.shape[1]), 0)
        lane = lax.broadcasted_iota(jnp.int32, (feats.shape[1], feats.shape[1]), 1)
        first = h * 2 * feat
        moved = (lane == key + feat) & (key >= first) & (key < first + feat)
        query = dot(feats, jnp.where(moved, 1.0, 0.0).astype(bf16)).astype(bf16)
        for b in range(rows // BLOCK):
            at = slice(b * BLOCK, (b + 1) * BLOCK)
            ahead = (b + 1) * BLOCK
            inner = dot_t(query[at], feats[:ahead])
            pair = 1.0 + inner * (0.25 + inner * (1.0 / 32.0))
            last = jnp.where(col <= row, pair[:, b * BLOCK :], 0.0)
            pair = jnp.concatenate([pair[:, : b * BLOCK], last], axis=1) if b else last
            near_ref[at, cols] = dot(pair.astype(bf16), kv_ref[:ahead, vcols])


def window_kernel(win, qf_ref, kv_ref, halo_ref, win_ref, qn_ref, sem):
    copy = pltpu.make_async_copy(qf_ref, qn_ref, sem)
    copy.start()
    copy.wait()
    seq = position()[3]
    rows = qn_ref.shape[0]
    heads = win_ref.shape[1] // 128
    head = 128
    halo = halo_ref.shape[0]
    span = halo + BLOCK
    blocks = rows // BLOCK
    row = lax.broadcasted_iota(jnp.int32, (BLOCK, span), 0)
    col = lax.broadcasted_iota(jnp.int32, (BLOCK, span), 1)
    causal = col <= row + halo
    for h in range(heads):
        cols = slice(h * head, (h + 1) * head)
        vcols = slice((heads + h) * head, (heads + h + 1) * head)
        keys = jnp.concatenate([halo_ref[:, cols], kv_ref[:, cols]], axis=0)
        values = jnp.concatenate([halo_ref[:, vcols], kv_ref[:, vcols]], axis=0)
        for b in range(blocks):
            at = slice(b * BLOCK, (b + 1) * BLOCK)
            scores = dot_t(qn_ref[at, cols], keys[b * BLOCK : b * BLOCK + span]) * (SCALE / head)
            least = jnp.maximum(span // BLOCK - win[h], span // BLOCK - 1 - (seq * blocks + b))
            allowed = causal & (col >= least * BLOCK)
            weights = jnp.where(allowed, jnp.exp(scores), 0.0).astype(bf16)
            win_ref[at, cols] = unit(dot(weights, values[b * BLOCK : b * BLOCK + span]))


def hidden_kernel(ours, theirs, near_ref, win_ref, high_ref, low_ref, keep_ref, away_ref, hidden):
    x, half, core, _ = position()
    mine, other = ours[...], theirs[...].astype(f32)
    head = mine.shape[1]
    rows = hidden.shape[1]
    for h in range(2):
        cols = slice(h * head, (h + 1) * head)
        state_high, state_low = halves(jnp.where(core == h, mine, other))
        high = high_ref[h]
        far = dot(high, state_high) + dot(low_ref[h], state_high) + dot(high, state_low)
        out = (unit(near_ref[:, cols] + far) + win_ref[:, cols]).astype(bf16)
        for g in range(N_TP):
            hidden[g, :, cols] = out[g * rows : (g + 1) * rows]
    for s in range(NX):
        group = lax.rem(x + s, NX) * 2
        keep_ref[s * rows : (s + 1) * rows] = hidden[group + half]
        away_ref[s * rows : (s + 1) * rows] = hidden[group + 1 - half]


def product_kernel(hidden_ref, w_ref, *outs):
    rows = outs[0].shape[0]
    product = dot(hidden_ref[...], w_ref[...]).astype(bf16)
    for s, out in enumerate(outs):
        out[...] = product[s * rows : (s + 1) * rows]


def prefix(mine, short, other, place, beside):
    x, h, y, z, c = place
    across = send(other, lambda x, h, y, z, c: (x, h, y, z ^ 1, 1 - c)).astype(f32)
    beyond = send(short, to_z(1)).astype(f32)
    got = send(other, to_core).astype(f32)
    total = mine + got + across + beyond
    add = (jnp.where(c == 0, mine, 0.0), jnp.where(c == 1, got, 0.0))
    before = jnp.where(z % 2 == 1, across + beyond, 0.0)
    total, before, add = lax.optimization_barrier((total, before, add))
    done = None
    for flip in (2, 4):
        part = send(total.astype(bf16), to_z(flip))
        if flip == 4:
            *behind, halo = done
            part, *behind = lax.optimization_barrier((part, *behind))
            done = (*behind, halo)
        part = part.astype(f32)
        before = before + jnp.where((z ^ flip) < z, part, 0.0)
        total, before = lax.optimization_barrier((total + part, before))
        if flip == 2:
            done = beside(total)
    short = total.astype(bf16)
    for steps in (1, 2, 3):
        before = before + send(short, to_y(steps)).astype(f32)
    theirs = send((before + add[0]).astype(bf16), to_core)
    ours = before + add[1]
    return ours, theirs, done


def shape(dims, kind):
    return jax.ShapeDtypeStruct(dims, kind)


def project(parts, wf, ww, tables):
    tok_rows = parts[0].shape[0]
    wide = 2 * ww.shape[2] // 3
    queries = shape((tok_rows, wide + 2 * wf.shape[0]), bf16)
    tail = shape(((WMAX - 1) * BLOCK, 2 * wide), bf16)
    return pl.pallas_call(
        project_kernel,
        out_shape=(
            queries,
            shape((tok_rows, 2 * wide), bf16),
            tail,
            shape((ROWS, wide // 2), f32),
            shape((ROWS, wide // 2), bf16),
            shape((ROWS, wide // 2), bf16),
        ),
        in_specs=[HBM] * (N_TP + 1) + [VMEM] * 2,
        out_specs=(HBM, VMEM, HBM, VMEM, VMEM, VMEM),
        scratch_shapes=[
            pltpu.VMEM((tok_rows, wf.shape[1]), bf16),
            pltpu.VMEM(wf.shape, bf16),
            pltpu.VMEM(queries.shape, bf16),
            pltpu.VMEM(tail.shape, bf16),
            pltpu.SemaphoreType.DMA((N_TP + 1,)),
        ],
        name="project",
        compiler_params=pltpu.CompilerParams(vmem_limit_bytes=LIMIT),
    )(*parts, wf, ww, tables.astype(bf16))


def near(qf, kv, tables):
    tok_rows, wide = kv.shape[0], kv.shape[1] // 2
    return pl.pallas_call(
        near_kernel,
        out_shape=(
            shape((tok_rows, wide), f32),
            shape((2, tok_rows, ROWS), bf16),
            shape((2, tok_rows, ROWS), bf16),
        ),
        in_specs=[HBM, VMEM, VMEM],
        out_specs=(VMEM,) * 3,
        scratch_shapes=[pltpu.VMEM(qf.shape, bf16), pltpu.SemaphoreType.DMA],
        name="near",
        compiler_params=pltpu.CompilerParams(vmem_limit_bytes=LIMIT),
    )(qf, kv, tables.astype(bf16))


def window(win_blocks, qf, kv, halo):
    return pl.pallas_call(
        window_kernel,
        out_shape=shape((kv.shape[0], kv.shape[1] // 2), f32),
        in_specs=[SMEM, HBM, VMEM, VMEM],
        out_specs=VMEM,
        scratch_shapes=[pltpu.VMEM(qf.shape, bf16), pltpu.SemaphoreType.DMA],
        name="window",
        compiler_params=pltpu.CompilerParams(vmem_limit_bytes=LIMIT),
    )(win_blocks, qf, kv, halo)


def hidden_rows(ours, theirs, near_out, win_out, high, low):
    tok_rows, wide = near_out.shape
    return pl.pallas_call(
        hidden_kernel,
        out_shape=(shape((tok_rows // 2, wide), bf16),) * 2,
        in_specs=[VMEM] * 6,
        out_specs=(VMEM,) * 2,
        scratch_shapes=[pltpu.VMEM((N_TP, tok_rows // N_TP, wide), bf16)],
        name="hidden",
        compiler_params=pltpu.CompilerParams(vmem_limit_bytes=LIMIT),
    )(ours, theirs, near_out, win_out, high, low)


def product(hidden, w_out):
    return pl.pallas_call(
        product_kernel,
        out_shape=(shape((hidden.shape[0] // NX, w_out.shape[1]), bf16),) * NX,
        in_specs=[VMEM] * 2,
        out_specs=(VMEM,) * NX,
        name="product",
        compiler_params=pltpu.CompilerParams(vmem_limit_bytes=LIMIT),
    )(hidden, w_out)


LIMIT = 12 * 2**20


def local(tokens, w_feature, w_window, w_out, win_blocks):
    model_width, head_count = w_feature.shape[:2]
    feat_dim = w_feature.shape[2] // 2
    seq, tp = lax.axis_index("seq"), lax.axis_index("tp")
    x, h, y, z, c = tp // 2, tp % 2, seq // (2 * NZ), seq // 2 % NZ, seq % 2

    other = send(tokens, to_half)
    parts = [tokens] + [send(tokens, to_x(s)) for s in (1, 3, 2)]
    w_out = w_out.reshape(-1, model_width)
    parts += [other] + [send(other, to_x(s)) for s in (1, 3, 2)]
    tables = feature_maps(feat_dim, head_count)
    qf, kv, tail, mine, short, theirs = project(
        parts, w_feature.transpose(1, 2, 0).reshape(-1, model_width), w_window.transpose(1, 0, 2), tables
    )

    def beside(total):
        early, kept, _ = lax.optimization_barrier((qf, tail, total))
        return *near(early, kv, tables), send(kept, to_next)

    ours, theirs, (near_out, high, low, halo) = prefix(mine, short, theirs, (x, h, y, z, c), beside)
    win_out = window(win_blocks, qf, kv, halo)
    keep, away = hidden_rows(ours, theirs, near_out, win_out, high, low)

    def summed(total, group):
        for steps in (1, 3, 2):
            total = total + send(group[steps], to_x(steps)).astype(f32)
        return total.astype(bf16)

    group = product(away, w_out)
    away, keep = lax.optimization_barrier((summed(group[0].astype(f32), group), keep))
    group = product(keep, w_out)
    total = lax.optimization_barrier(group[0].astype(f32) + send(away, to_half).astype(f32))
    return summed(total, group)


def solution(mesh):
    in_specs = (P("seq", "tp"), P(None, "tp", None), P(None, "tp", None), P("tp", None, None), P("tp"))
    return jax.shard_map(local, mesh=mesh, in_specs=in_specs, out_specs=P(("seq", "tp"), None), check_vma=False)
```

```python
import jax
import jax.numpy as jnp
import numpy as np
from jax import lax
from jax.experimental import pallas as pl
from jax.experimental.pallas import tpu as pltpu
from jax.sharding import PartitionSpec as P

BLOCK = 128
WMAX = 4
NX, NY, NZ = 4, 4, 8
N_TP = 8
EPS = 1e-06
SCALE = 12.0
bf16, f32 = jnp.bfloat16, jnp.float32


def pairs(move):
    out = []
    for x in range(NX):
        for h in range(2):
            for y in range(NY):
                for z in range(NZ):
                    for c in range(2):
                        to = move(x, h, y, z, c)
                        if to is not None:
                            tx, th, ty, tz, tc = to
                            source = ((y * NZ + z) * 2 + c) * N_TP + x * 2 + h
                            target = ((ty * NZ + tz) * 2 + tc) * N_TP + (tx % NX) * 2 + th
                            out.append((source, target))
    return out


def send(value, move):
    return lax.ppermute(value, ("seq", "tp"), pairs(move))


def to_x(steps):
    return lambda x, h, y, z, c: (x + steps, h, y, z, c)


def to_half(x, h, y, z, c):
    return (x, 1 - h, y, z, c)


def to_core(x, h, y, z, c):
    return (x, h, y, z, 1 - c)


def to_z(flip):
    return lambda x, h, y, z, c: (x, h, y, z ^ flip, c)


def to_y(steps):
    return lambda x, h, y, z, c: (x, h, y + steps, z, c) if y + steps < NY else None


def to_next(x, h, y, z, c):
    place = (y * NZ + z) * 2 + c + 1
    if place == NY * NZ * 2:
        return None
    return (x, h, place // (2 * NZ), place // 2 % NZ, place % 2)


ROWS = 160
VMEM = pl.BlockSpec(memory_space=pltpu.VMEM)
HBM = pl.BlockSpec(memory_space=pltpu.HBM)
SMEM = pl.BlockSpec(memory_space=pltpu.SMEM)


def feature_maps(feat_dim, heads):
    width = heads * 2 * feat_dim
    tables = np.zeros((heads, 4, ROWS, 2 * width), np.float32)
    at = 0
    for i in range(feat_dim):
        for j in range(i, feat_dim):
            for head in range(heads):
                query, key = head * 2 * feat_dim, (head * 2 + 1) * feat_dim
                tables[head, 0, at, query + i] = 1.0 / 32.0 if i == j else 1.0 / 16.0
                tables[head, 1, at, query + j] = 1.0
                tables[head, 2, at, key + i] = 1.0
                tables[head, 3, at, key + j] = 1.0
            at += 1
    for i in range(feat_dim):
        for head in range(heads):
            query, key = head * 2 * feat_dim, (head * 2 + 1) * feat_dim
            tables[head, 0, at, query + i] = 0.25
            tables[head, 2, at, key + i] = 1.0
        tables[:, 1::2, at, width] = 1.0
        at += 1
    tables[:, :, at, width] = 1.0
    return tables


def dot(a, b):
    return jnp.dot(a, b, preferred_element_type=f32)


def dot_t(a, b):
    return lax.dot_general(a, b, (((1,), (1,)), ((), ())), preferred_element_type=f32)


def unit(v):
    return v * lax.rsqrt(jnp.mean(v * v, axis=-1, keepdims=True) + EPS)


def halves(v):
    high = v.astype(bf16)
    return high, (v - high.astype(f32)).astype(bf16)


def position():
    seq, tp = lax.axis_index("seq"), lax.axis_index("tp")
    return lax.div(tp, 2), lax.rem(tp, 2), lax.rem(seq, 2), seq


def contract(parts, wf, ww, mine):
    x, half, _, _ = position()
    side = half if mine else 1 - half
    width = parts[0].shape[1]
    head = ww.shape[2] // 3
    tokens = jnp.concatenate([part[...] for part in parts], axis=1)
    owners = [lax.rem(x + NX - s, NX) * 2 + side for s in (0, 1, 3, 2)]
    rows = [pl.ds(pl.multiple_of(owner * width, width), width) for owner in owners]

    def columns(kind):
        cols = slice(kind * head, (kind + 1) * head)
        weight = [jnp.concatenate([ww[h, r, cols] for h in range(2)], axis=1) for r in rows]
        return dot(tokens, jnp.concatenate(weight, axis=0))

    return dot_t(tokens, jnp.concatenate([wf[:, r] for r in rows], axis=1)), columns


def own_kernel(*refs):
    parts = refs[:NX]
    wf, ww, feats_ref, sums_ref = refs[NX:]
    feats, columns = contract(parts, wf, ww, True)
    feats_ref[...] = feats
    for kind in range(3):
        sums_ref[kind] = columns(kind)


def project_kernel(*refs):
    parts = refs[:NX]
    wf, ww, table, own_feats, own_sums, qf_ref, kv_ref, tail_ref, mine_ref, short_ref, other_ref, qf, tail, sems = refs[NX:]
    core = position()[2]
    head = ww.shape[2] // 3
    feats, columns = contract(parts, wf, ww, False)
    feats = (feats + own_feats[...]).astype(bf16)
    ones = lax.broadcasted_iota(jnp.int32, feats.shape, 1) == 0
    feats = jnp.concatenate([feats, jnp.where(ones, 1.0, 0.0).astype(bf16)], axis=1)
    qf[:, 2 * head :] = feats
    first_tail = kv_ref.shape[0] - tail.shape[0]
    leave = [pltpu.make_async_copy(tail, tail_ref, sems.at[0]), pltpu.make_async_copy(qf, qf_ref, sems.at[1])]
    for kind in (2, 1, 0):
        out = (columns(kind) + own_sums[kind]).astype(bf16)
        if kind == 2:
            values = out
            kv_ref[:, 2 * head :] = out
            tail[:, 2 * head :] = out[first_tail:]
            continue
        for h in range(2):
            cols = slice(h * head, (h + 1) * head)
            normed = unit(out[:, cols].astype(f32)).astype(bf16)
            if kind == 1:
                kv_ref[:, cols] = normed
                tail[:, cols] = normed[first_tail:]
            else:
                qf[:, cols] = normed
        leave[1 - kind].start()
    states = []
    for h in range(2):
        left = dot_t(table[h, 2], feats)
        right = dot_t(table[h, 3], feats)
        high, low = halves(left * right)
        v = values[:, h * head : (h + 1) * head]
        states.append(dot(high, v) + dot(low, v))
    mine = jnp.where(core == 0, states[0], states[1])
    mine_ref[...] = mine
    short_ref[...] = mine.astype(bf16)
    other_ref[...] = jnp.where(core == 0, states[1], states[0]).astype(bf16)
    for copy in leave:
        copy.wait()


def near_kernel(qf_ref, kv_ref, table, near_ref, high_ref, low_ref, qn_ref, sem):
    copy = pltpu.make_async_copy(qf_ref, qn_ref, sem)
    copy.start()
    copy.wait()
    rows = qn_ref.shape[0]
    heads = near_ref.shape[1] // 128
    head = 128
    feats = qn_ref[:, heads * head :]
    feat = feats.shape[1] // (4 * heads)
    row = lax.broadcasted_iota(jnp.int32, (BLOCK, BLOCK), 0)
    col = lax.broadcasted_iota(jnp.int32, (BLOCK, BLOCK), 1)
    for h in range(heads):
        cols = slice(h * head, (h + 1) * head)
        vcols = slice((heads + h) * head, (heads + h + 1) * head)
        left = dot_t(feats, table[h, 0])
        right = dot_t(feats, table[h, 1])
        high, low = halves(left * right)
        high_ref[h] = high
        low_ref[h] = low
        key = lax.broadcasted_iota(jnp.int32, (feats.shape[1], feats.shape[1]), 0)
        lane = lax.broadcasted_iota(jnp.int32, (feats.shape[1], feats.shape[1]), 1)
        first = h * 2 * feat
        moved = (lane == key + feat) & (key >= first) & (key < first + feat)
        query = dot(feats, jnp.where(moved, 1.0, 0.0).astype(bf16)).astype(bf16)
        for b in range(rows // BLOCK):
            at = slice(b * BLOCK, (b + 1) * BLOCK)
            ahead = (b + 1) * BLOCK
            inner = dot_t(query[at], feats[:ahead])
            pair = 1.0 + inner * (0.25 + inner * (1.0 / 32.0))
            last = jnp.where(col <= row, pair[:, b * BLOCK :], 0.0)
            pair = jnp.concatenate([pair[:, : b * BLOCK], last], axis=1) if b else last
            near_ref[at, cols] = dot(pair.astype(bf16), kv_ref[:ahead, vcols])


def window_kernel(win, qf_ref, kv_ref, halo_ref, win_ref, qn_ref, sem):
    copy = pltpu.make_async_copy(qf_ref, qn_ref, sem)
    copy.start()
    copy.wait()
    seq = position()[3]
    rows = qn_ref.shape[0]
    heads = win_ref.shape[1] // 128
    head = 128
    halo = halo_ref.shape[0]
    span = halo + BLOCK
    blocks = rows // BLOCK
    row = lax.broadcasted_iota(jnp.int32, (BLOCK, span), 0)
    col = lax.broadcasted_iota(jnp.int32, (BLOCK, span), 1)
    causal = col <= row + halo
    for h in range(heads):
        cols = slice(h * head, (h + 1) * head)
        vcols = slice((heads + h) * head, (heads + h + 1) * head)
        keys = jnp.concatenate([halo_ref[:, cols], kv_ref[:, cols]], axis=0)
        values = jnp.concatenate([halo_ref[:, vcols], kv_ref[:, vcols]], axis=0)
        for b in range(blocks):
            at = slice(b * BLOCK, (b + 1) * BLOCK)
            scores = dot_t(qn_ref[at, cols], keys[b * BLOCK : b * BLOCK + span]) * (SCALE / head)
            least = jnp.maximum(span // BLOCK - win[h], span // BLOCK - 1 - (seq * blocks + b))
            allowed = causal & (col >= least * BLOCK)
            weights = jnp.where(allowed, jnp.exp(scores), 0.0).astype(bf16)
            win_ref[at, cols] = unit(dot(weights, values[b * BLOCK : b * BLOCK + span]))


def hidden_kernel(ours, theirs, near_ref, win_ref, high_ref, low_ref, keep_ref, away_ref, hidden):
    x, half, core, _ = position()
    mine, other = ours[...], theirs[...].astype(f32)
    head = mine.shape[1]
    rows = hidden.shape[1]
    for h in range(2):
        cols = slice(h * head, (h + 1) * head)
        state_high, state_low = halves(jnp.where(core == h, mine, other))
        high = high_ref[h]
        far = dot(high, state_high) + dot(low_ref[h], state_high) + dot(high, state_low)
        out = (unit(near_ref[:, cols] + far) + win_ref[:, cols]).astype(bf16)
        for g in range(N_TP):
            hidden[g, :, cols] = out[g * rows : (g + 1) * rows]
    for s in range(NX):
        group = lax.rem(x + s, NX) * 2
        keep_ref[s * rows : (s + 1) * rows] = hidden[group + half]
        away_ref[s * rows : (s + 1) * rows] = hidden[group + 1 - half]


def product_kernel(hidden_ref, w_ref, *outs):
    rows = outs[0].shape[0]
    product = dot(hidden_ref[...], w_ref[...]).astype(bf16)
    for s, out in enumerate(outs):
        out[...] = product[s * rows : (s + 1) * rows]


def prefix(mine, short, other, place, beside):
    x, h, y, z, c = place
    across = send(other, lambda x, h, y, z, c: (x, h, y, z ^ 1, 1 - c)).astype(f32)
    beyond = send(short, to_z(1)).astype(f32)
    got = send(other, to_core).astype(f32)
    total = mine + got + across + beyond
    add = (jnp.where(c == 0, mine, 0.0), jnp.where(c == 1, got, 0.0))
    before = jnp.where(z % 2 == 1, across + beyond, 0.0)
    total, before, add = lax.optimization_barrier((total, before, add))
    done = None
    for flip in (2, 4):
        part = send(total.astype(bf16), to_z(flip))
        if flip == 4:
            *behind, halo = done
            part, *behind = lax.optimization_barrier((part, *behind))
            done = (*behind, halo)
        part = part.astype(f32)
        before = before + jnp.where((z ^ flip) < z, part, 0.0)
        total, before = lax.optimization_barrier((total + part, before))
        if flip == 2:
            done = beside(total)
    short = total.astype(bf16)
    for steps in (1, 2, 3):
        before = before + send(short, to_y(steps)).astype(f32)
    theirs = send((before + add[0]).astype(bf16), to_core)
    ours = before + add[1]
    return ours, theirs, done


def shape(dims, kind):
    return jax.ShapeDtypeStruct(dims, kind)


def own_products(parts, wf, ww):
    tok_rows = parts[0].shape[0]
    return pl.pallas_call(
        own_kernel,
        out_shape=(shape((tok_rows, wf.shape[0]), f32), shape((3, tok_rows, 2 * ww.shape[2] // 3), f32)),
        in_specs=[VMEM] * (NX + 2),
        out_specs=(VMEM,) * 2,
        name="own",
        compiler_params=pltpu.CompilerParams(vmem_limit_bytes=LIMIT),
    )(*parts, wf, ww)


def project(parts, wf, ww, tables, own):
    tok_rows = parts[0].shape[0]
    wide = 2 * ww.shape[2] // 3
    queries = shape((tok_rows, wide + 2 * wf.shape[0]), bf16)
    tail = shape(((WMAX - 1) * BLOCK, 2 * wide), bf16)
    return pl.pallas_call(
        project_kernel,
        out_shape=(
            queries,
            shape((tok_rows, 2 * wide), bf16),
            tail,
            shape((ROWS, wide // 2), f32),
            shape((ROWS, wide // 2), bf16),
            shape((ROWS, wide // 2), bf16),
        ),
        in_specs=[VMEM] * (NX + 5),
        out_specs=(HBM, VMEM, HBM, VMEM, VMEM, VMEM),
        scratch_shapes=[
            pltpu.VMEM(queries.shape, bf16),
            pltpu.VMEM(tail.shape, bf16),
            pltpu.SemaphoreType.DMA((2,)),
        ],
        name="project",
        compiler_params=pltpu.CompilerParams(vmem_limit_bytes=LIMIT),
    )(*parts, wf, ww, tables.astype(bf16), *own)


def near(qf, kv, tables):
    tok_rows, wide = kv.shape[0], kv.shape[1] // 2
    return pl.pallas_call(
        near_kernel,
        out_shape=(
            shape((tok_rows, wide), f32),
            shape((2, tok_rows, ROWS), bf16),
            shape((2, tok_rows, ROWS), bf16),
        ),
        in_specs=[HBM, VMEM, VMEM],
        out_specs=(VMEM,) * 3,
        scratch_shapes=[pltpu.VMEM(qf.shape, bf16), pltpu.SemaphoreType.DMA],
        name="near",
        compiler_params=pltpu.CompilerParams(vmem_limit_bytes=LIMIT),
    )(qf, kv, tables.astype(bf16))


def window(win_blocks, qf, kv, halo):
    return pl.pallas_call(
        window_kernel,
        out_shape=shape((kv.shape[0], kv.shape[1] // 2), f32),
        in_specs=[SMEM, HBM, VMEM, VMEM],
        out_specs=VMEM,
        scratch_shapes=[pltpu.VMEM(qf.shape, bf16), pltpu.SemaphoreType.DMA],
        name="window",
        compiler_params=pltpu.CompilerParams(vmem_limit_bytes=LIMIT),
    )(win_blocks, qf, kv, halo)


def hidden_rows(ours, theirs, near_out, win_out, high, low):
    tok_rows, wide = near_out.shape
    return pl.pallas_call(
        hidden_kernel,
        out_shape=(shape((tok_rows // 2, wide), bf16),) * 2,
        in_specs=[VMEM] * 6,
        out_specs=(VMEM,) * 2,
        scratch_shapes=[pltpu.VMEM((N_TP, tok_rows // N_TP, wide), bf16)],
        name="hidden",
        compiler_params=pltpu.CompilerParams(vmem_limit_bytes=LIMIT),
    )(ours, theirs, near_out, win_out, high, low)


def product(hidden, w_out):
    return pl.pallas_call(
        product_kernel,
        out_shape=(shape((hidden.shape[0] // NX, w_out.shape[1]), bf16),) * NX,
        in_specs=[VMEM] * 2,
        out_specs=(VMEM,) * NX,
        name="product",
        compiler_params=pltpu.CompilerParams(vmem_limit_bytes=LIMIT),
    )(hidden, w_out)


LIMIT = 12 * 2**20


def local(tokens, w_feature, w_window, w_out, win_blocks):
    model_width, head_count = w_feature.shape[:2]
    feat_dim = w_feature.shape[2] // 2
    seq, tp = lax.axis_index("seq"), lax.axis_index("tp")
    x, h, y, z, c = tp // 2, tp % 2, seq // (2 * NZ), seq // 2 % NZ, seq % 2

    other = send(tokens, to_half)
    parts = [tokens] + [send(tokens, to_x(s)) for s in (1, 3, 2)]
    w_out = w_out.reshape(-1, model_width)
    parts += [other] + [send(other, to_x(s)) for s in (1, 3, 2)]
    tables = feature_maps(feat_dim, head_count)
    wf, ww = w_feature.transpose(1, 2, 0).reshape(-1, model_width), w_window.transpose(1, 0, 2)
    own = own_products(parts[:NX], wf, ww)
    qf, kv, tail, mine, short, theirs = project(parts[NX:], wf, ww, tables, own)

    def beside(total):
        early, kept, _ = lax.optimization_barrier((qf, tail, total))
        return *near(early, kv, tables), send(kept, to_next)

    ours, theirs, (near_out, high, low, halo) = prefix(mine, short, theirs, (x, h, y, z, c), beside)
    win_out = window(win_blocks, qf, kv, halo)
    keep, away = hidden_rows(ours, theirs, near_out, win_out, high, low)

    def summed(total, group):
        for steps in (1, 3, 2):
            total = total + send(group[steps], to_x(steps)).astype(f32)
        return total.astype(bf16)

    group = product(away, w_out)
    away, keep = lax.optimization_barrier((summed(group[0].astype(f32), group), keep))
    group = product(keep, w_out)
    total = lax.optimization_barrier(group[0].astype(f32) + send(away, to_half).astype(f32))
    return summed(total, group)


def solution(mesh):
    in_specs = (P("seq", "tp"), P(None, "tp", None), P(None, "tp", None), P("tp", None, None), P("tp"))
    return jax.shard_map(local, mesh=mesh, in_specs=in_specs, out_specs=P(("seq", "tp"), None), check_vma=False)
```

```python
import jax
import jax.numpy as jnp
import numpy as np
from jax import lax
from jax.experimental import pallas as pl
from jax.experimental.pallas import tpu as pltpu
from jax.sharding import PartitionSpec as P

BLOCK = 128
WMAX = 4
NX, NY, NZ = 4, 4, 8
N_TP = 8
EPS = 1e-06
SCALE = 12.0
bf16, f32 = jnp.bfloat16, jnp.float32


def pairs(move):
    out = []
    for x in range(NX):
        for h in range(2):
            for y in range(NY):
                for z in range(NZ):
                    for c in range(2):
                        to = move(x, h, y, z, c)
                        if to is not None:
                            tx, th, ty, tz, tc = to
                            source = ((y * NZ + z) * 2 + c) * N_TP + x * 2 + h
                            target = ((ty * NZ + tz) * 2 + tc) * N_TP + (tx % NX) * 2 + th
                            out.append((source, target))
    return out


def send(value, move):
    return lax.ppermute(value, ("seq", "tp"), pairs(move))


def to_x(steps):
    return lambda x, h, y, z, c: (x + steps, h, y, z, c)


def to_half(x, h, y, z, c):
    return (x, 1 - h, y, z, c)


def to_core(x, h, y, z, c):
    return (x, h, y, z, 1 - c)


def to_z(flip):
    return lambda x, h, y, z, c: (x, h, y, z ^ flip, c)


def to_y(steps):
    return lambda x, h, y, z, c: (x, h, y + steps, z, c) if y + steps < NY else None


def to_next(x, h, y, z, c):
    place = (y * NZ + z) * 2 + c + 1
    if place == NY * NZ * 2:
        return None
    return (x, h, place // (2 * NZ), place // 2 % NZ, place % 2)


ROWS = 160
VMEM = pl.BlockSpec(memory_space=pltpu.VMEM)
HBM = pl.BlockSpec(memory_space=pltpu.HBM)
SMEM = pl.BlockSpec(memory_space=pltpu.SMEM)


def feature_maps(feat_dim, heads):
    width = heads * 2 * feat_dim
    tables = np.zeros((heads, 4, ROWS, 2 * width), np.float32)
    at = 0
    for i in range(feat_dim):
        for j in range(i, feat_dim):
            for head in range(heads):
                query, key = head * 2 * feat_dim, (head * 2 + 1) * feat_dim
                tables[head, 0, at, query + i] = 1.0 / 32.0 if i == j else 1.0 / 16.0
                tables[head, 1, at, query + j] = 1.0
                tables[head, 2, at, key + i] = 1.0
                tables[head, 3, at, key + j] = 1.0
            at += 1
    for i in range(feat_dim):
        for head in range(heads):
            query, key = head * 2 * feat_dim, (head * 2 + 1) * feat_dim
            tables[head, 0, at, query + i] = 0.25
            tables[head, 2, at, key + i] = 1.0
        tables[:, 1::2, at, width] = 1.0
        at += 1
    tables[:, :, at, width] = 1.0
    return tables


def dot(a, b):
    return jnp.dot(a, b, preferred_element_type=f32)


def dot_t(a, b):
    return lax.dot_general(a, b, (((1,), (1,)), ((), ())), preferred_element_type=f32)


def unit(v):
    return v * lax.rsqrt(jnp.mean(v * v, axis=-1, keepdims=True) + EPS)


def halves(v):
    high = v.astype(bf16)
    return high, (v - high.astype(f32)).astype(bf16)


def position():
    seq, tp = lax.axis_index("seq"), lax.axis_index("tp")
    return lax.div(tp, 2), lax.rem(tp, 2), lax.rem(seq, 2), seq


def contract(parts, wf, ww, mine):
    x, half, _, _ = position()
    side = half if mine else 1 - half
    width = parts[0].shape[1]
    head = ww.shape[2] // 3
    tokens = jnp.concatenate([part[...] for part in parts], axis=1)
    owners = [lax.rem(x + NX - s, NX) * 2 + side for s in (0, 1, 3, 2)]
    rows = [pl.ds(pl.multiple_of(owner * width, width), width) for owner in owners]

    def columns(kind):
        cols = slice(kind * head, (kind + 1) * head)
        weight = [jnp.concatenate([ww[h, r, cols] for h in range(2)], axis=1) for r in rows]
        return dot(tokens, jnp.concatenate(weight, axis=0))

    return dot_t(tokens, jnp.concatenate([wf[:, r] for r in rows], axis=1)), columns


def own_kernel(*refs):
    parts = refs[:NX]
    wf, ww, feats_ref, sums_ref = refs[NX:]
    feats, columns = contract(parts, wf, ww, True)
    feats_ref[...] = feats
    for kind in range(3):
        sums_ref[kind] = columns(kind)


def project_kernel(*refs):
    parts = refs[:NX]
    wf, ww, table, own_feats, own_sums, qf_ref, kv_ref, tail_ref, mine_ref, short_ref, other_ref, qf, tail, sems = refs[NX:]
    core = position()[2]
    head = ww.shape[2] // 3
    feats, columns = contract(parts, wf, ww, False)
    feats = (feats + own_feats[...]).astype(bf16)
    ones = lax.broadcasted_iota(jnp.int32, feats.shape, 1) == 0
    feats = jnp.concatenate([feats, jnp.where(ones, 1.0, 0.0).astype(bf16)], axis=1)
    qf[:, 2 * head :] = feats
    first_tail = kv_ref.shape[0] - tail.shape[0]
    leave = [pltpu.make_async_copy(tail, tail_ref, sems.at[0]), pltpu.make_async_copy(qf, qf_ref, sems.at[1])]
    for kind in (2, 1, 0):
        out = (columns(kind) + own_sums[kind]).astype(bf16)
        if kind == 2:
            values = out
            kv_ref[:, 2 * head :] = out
            tail[:, 2 * head :] = out[first_tail:]
            continue
        for h in range(2):
            cols = slice(h * head, (h + 1) * head)
            normed = unit(out[:, cols].astype(f32)).astype(bf16)
            if kind == 1:
                kv_ref[:, cols] = normed
                tail[:, cols] = normed[first_tail:]
            else:
                qf[:, cols] = normed
        leave[1 - kind].start()
    states = []
    for h in range(2):
        left = dot_t(table[h, 2], feats)
        right = dot_t(table[h, 3], feats)
        high, low = halves(left * right)
        v = values[:, h * head : (h + 1) * head]
        states.append(dot(high, v) + dot(low, v))
    mine = jnp.where(core == 0, states[0], states[1])
    mine_ref[...] = mine
    short_ref[...] = mine.astype(bf16)
    other_ref[...] = jnp.where(core == 0, states[1], states[0]).astype(bf16)
    for copy in leave:
        copy.wait()


def near_kernel(qf_ref, kv_ref, table, near_ref, map_ref, qn_ref, sem):
    copy = pltpu.make_async_copy(qf_ref, qn_ref, sem)
    copy.start()
    copy.wait()
    rows = qn_ref.shape[0]
    heads = near_ref.shape[1] // 128
    head = 128
    feats = qn_ref[:, heads * head :]
    feat = feats.shape[1] // (4 * heads)
    row = lax.broadcasted_iota(jnp.int32, (BLOCK, BLOCK), 0)
    col = lax.broadcasted_iota(jnp.int32, (BLOCK, BLOCK), 1)
    for h in range(heads):
        cols = slice(h * head, (h + 1) * head)
        vcols = slice((heads + h) * head, (heads + h + 1) * head)
        left = dot_t(feats, table[h, 0])
        right = dot_t(feats, table[h, 1])
        map_ref[h] = (left * right).astype(bf16)
        key = lax.broadcasted_iota(jnp.int32, (feats.shape[1], feats.shape[1]), 0)
        lane = lax.broadcasted_iota(jnp.int32, (feats.shape[1], feats.shape[1]), 1)
        first = h * 2 * feat
        moved = (lane == key + feat) & (key >= first) & (key < first + feat)
        query = dot(feats, jnp.where(moved, 1.0, 0.0).astype(bf16)).astype(bf16)
        for b in range(rows // BLOCK):
            at = slice(b * BLOCK, (b + 1) * BLOCK)
            ahead = (b + 1) * BLOCK
            inner = dot_t(query[at], feats[:ahead])
            pair = 1.0 + inner * (0.25 + inner * (1.0 / 32.0))
            last = jnp.where(col <= row, pair[:, b * BLOCK :], 0.0)
            pair = jnp.concatenate([pair[:, : b * BLOCK], last], axis=1) if b else last
            near_ref[at, cols] = dot(pair.astype(bf16), kv_ref[:ahead, vcols])


def window_kernel(win, qf_ref, kv_ref, halo_ref, win_ref, qn_ref, sem):
    copy = pltpu.make_async_copy(qf_ref, qn_ref, sem)
    copy.start()
    copy.wait()
    seq = position()[3]
    rows = qn_ref.shape[0]
    heads = win_ref.shape[1] // 128
    head = 128
    halo = halo_ref.shape[0]
    span = halo + BLOCK
    blocks = rows // BLOCK
    row = lax.broadcasted_iota(jnp.int32, (BLOCK, span), 0)
    col = lax.broadcasted_iota(jnp.int32, (BLOCK, span), 1)
    causal = col <= row + halo
    for h in range(heads):
        cols = slice(h * head, (h + 1) * head)
        vcols = slice((heads + h) * head, (heads + h + 1) * head)
        keys = jnp.concatenate([halo_ref[:, cols], kv_ref[:, cols]], axis=0)
        values = jnp.concatenate([halo_ref[:, vcols], kv_ref[:, vcols]], axis=0)
        for b in range(blocks):
            at = slice(b * BLOCK, (b + 1) * BLOCK)
            scores = dot_t(qn_ref[at, cols], keys[b * BLOCK : b * BLOCK + span]) * (SCALE / head)
            least = jnp.maximum(span // BLOCK - win[h], span // BLOCK - 1 - (seq * blocks + b))
            allowed = causal & (col >= least * BLOCK)
            weights = jnp.where(allowed, jnp.exp(scores), 0.0).astype(bf16)
            win_ref[at, cols] = unit(dot(weights, values[b * BLOCK : b * BLOCK + span]))


def hidden_kernel(ours, theirs, near_ref, win_ref, map_ref, keep_ref, away_ref, hidden):
    x, half, core, _ = position()
    mine, other = ours[...], theirs[...].astype(f32)
    head = mine.shape[1]
    rows = hidden.shape[1]
    for h in range(2):
        cols = slice(h * head, (h + 1) * head)
        state_high, state_low = halves(jnp.where(core == h, mine, other))
        far = dot(map_ref[h], state_high) + dot(map_ref[h], state_low)
        out = (unit(near_ref[:, cols] + far) + win_ref[:, cols]).astype(bf16)
        for g in range(N_TP):
            hidden[g, :, cols] = out[g * rows : (g + 1) * rows]
    for s in range(NX):
        group = lax.rem(x + s, NX) * 2
        keep_ref[s * rows : (s + 1) * rows] = hidden[group + half]
        away_ref[s * rows : (s + 1) * rows] = hidden[group + 1 - half]


def product_kernel(hidden_ref, w_ref, *outs):
    rows = outs[0].shape[0]
    product = dot(hidden_ref[...], w_ref[...]).astype(bf16)
    for s, out in enumerate(outs):
        out[...] = product[s * rows : (s + 1) * rows]


def prefix(mine, short, other, place, attend, hand_on):
    x, h, y, z, c = place
    across = send(other, lambda x, h, y, z, c: (x, h, y, z ^ 1, 1 - c)).astype(f32)
    beyond = send(short, to_z(1)).astype(f32)
    got = send(other, to_core).astype(f32)
    total = mine + got + across + beyond
    add = (jnp.where(c == 0, mine, 0.0), jnp.where(c == 1, got, 0.0))
    before = jnp.where(z % 2 == 1, across + beyond, 0.0)
    total, before, add = lax.optimization_barrier((total, before, add))
    for flip in (2, 4):
        part = send(total.astype(bf16), to_z(flip))
        if flip == 2:
            part, *behind = lax.optimization_barrier((part, *attend(total)))
        else:
            halo = hand_on(total)
        part = part.astype(f32)
        before = before + jnp.where((z ^ flip) < z, part, 0.0)
        total, before = lax.optimization_barrier((total + part, before))
    short = total.astype(bf16)
    for steps in (1, 2, 3):
        before = before + send(short, to_y(steps)).astype(f32)
    theirs = send((before + add[0]).astype(bf16), to_core)
    ours = before + add[1]
    return ours, theirs, behind, halo


def shape(dims, kind):
    return jax.ShapeDtypeStruct(dims, kind)


def own_products(parts, wf, ww):
    tok_rows = parts[0].shape[0]
    return pl.pallas_call(
        own_kernel,
        out_shape=(shape((tok_rows, wf.shape[0]), f32), shape((3, tok_rows, 2 * ww.shape[2] // 3), f32)),
        in_specs=[VMEM] * (NX + 2),
        out_specs=(VMEM,) * 2,
        name="own",
        compiler_params=pltpu.CompilerParams(vmem_limit_bytes=LIMIT),
    )(*parts, wf, ww)


def project(parts, wf, ww, tables, own):
    tok_rows = parts[0].shape[0]
    wide = 2 * ww.shape[2] // 3
    queries = shape((tok_rows, wide + 2 * wf.shape[0]), bf16)
    tail = shape(((WMAX - 1) * BLOCK, 2 * wide), bf16)
    return pl.pallas_call(
        project_kernel,
        out_shape=(
            queries,
            shape((tok_rows, 2 * wide), bf16),
            tail,
            shape((ROWS, wide // 2), f32),
            shape((ROWS, wide // 2), bf16),
            shape((ROWS, wide // 2), bf16),
        ),
        in_specs=[VMEM] * (NX + 5),
        out_specs=(HBM, VMEM, HBM, VMEM, VMEM, VMEM),
        scratch_shapes=[
            pltpu.VMEM(queries.shape, bf16),
            pltpu.VMEM(tail.shape, bf16),
            pltpu.SemaphoreType.DMA((2,)),
        ],
        name="project",
        compiler_params=pltpu.CompilerParams(vmem_limit_bytes=LIMIT),
    )(*parts, wf, ww, tables.astype(bf16), *own)


def near(qf, kv, tables):
    tok_rows, wide = kv.shape[0], kv.shape[1] // 2
    return pl.pallas_call(
        near_kernel,
        out_shape=(
            shape((tok_rows, wide), f32),
            shape((2, tok_rows, ROWS), bf16),
        ),
        in_specs=[HBM, VMEM, VMEM],
        out_specs=(VMEM,) * 2,
        scratch_shapes=[pltpu.VMEM(qf.shape, bf16), pltpu.SemaphoreType.DMA],
        name="near",
        compiler_params=pltpu.CompilerParams(vmem_limit_bytes=LIMIT),
    )(qf, kv, tables.astype(bf16))


def window(win_blocks, qf, kv, halo):
    return pl.pallas_call(
        window_kernel,
        out_shape=shape((kv.shape[0], kv.shape[1] // 2), f32),
        in_specs=[SMEM, HBM, VMEM, VMEM],
        out_specs=VMEM,
        scratch_shapes=[pltpu.VMEM(qf.shape, bf16), pltpu.SemaphoreType.DMA],
        name="window",
        compiler_params=pltpu.CompilerParams(vmem_limit_bytes=LIMIT),
    )(win_blocks, qf, kv, halo)


def hidden_rows(ours, theirs, near_out, win_out, query_map):
    tok_rows, wide = near_out.shape
    return pl.pallas_call(
        hidden_kernel,
        out_shape=(shape((tok_rows // 2, wide), bf16),) * 2,
        in_specs=[VMEM] * 5,
        out_specs=(VMEM,) * 2,
        scratch_shapes=[pltpu.VMEM((N_TP, tok_rows // N_TP, wide), bf16)],
        name="hidden",
        compiler_params=pltpu.CompilerParams(vmem_limit_bytes=LIMIT),
    )(ours, theirs, near_out, win_out, query_map)


def product(hidden, w_out):
    return pl.pallas_call(
        product_kernel,
        out_shape=(shape((hidden.shape[0] // NX, w_out.shape[1]), bf16),) * NX,
        in_specs=[VMEM] * 2,
        out_specs=(VMEM,) * NX,
        name="product",
        compiler_params=pltpu.CompilerParams(vmem_limit_bytes=LIMIT),
    )(hidden, w_out)


LIMIT = 12 * 2**20


def local(tokens, w_feature, w_window, w_out, win_blocks):
    model_width, head_count = w_feature.shape[:2]
    feat_dim = w_feature.shape[2] // 2
    seq, tp = lax.axis_index("seq"), lax.axis_index("tp")
    x, h, y, z, c = tp // 2, tp % 2, seq // (2 * NZ), seq // 2 % NZ, seq % 2

    other = send(tokens, to_half)
    parts = [tokens] + [send(tokens, to_x(s)) for s in (1, 3, 2)]
    w_out = w_out.reshape(-1, model_width)
    parts += [other] + [send(other, to_x(s)) for s in (1, 3, 2)]
    tables = feature_maps(feat_dim, head_count)
    wf, ww = w_feature.transpose(1, 2, 0).reshape(-1, model_width), w_window.transpose(1, 0, 2)
    own = own_products(parts[:NX], wf, ww)
    qf, kv, tail, mine, short, theirs = project(parts[NX:], wf, ww, tables, own)

    def attend(total):
        return near(lax.optimization_barrier((qf, total))[0], kv, tables)

    def hand_on(total):
        return send(lax.optimization_barrier((tail, total))[0], to_next)

    ours, theirs, (near_out, query_map), halo = prefix(mine, short, theirs, (x, h, y, z, c), attend, hand_on)
    win_out = window(win_blocks, qf, kv, halo)
    keep, away = hidden_rows(ours, theirs, near_out, win_out, query_map)

    def summed(total, group):
        for steps in (2, 3, 1):
            total = total + send(group[steps], to_x(steps)).astype(f32)
        return total.astype(bf16)

    group = product(away, w_out)
    away, keep = lax.optimization_barrier((summed(group[0].astype(f32), group), keep))
    group = product(keep, w_out)
    total = lax.optimization_barrier(group[0].astype(f32) + send(away, to_half).astype(f32))
    return summed(total, group)


def solution(mesh):
    in_specs = (P("seq", "tp"), P(None, "tp", None), P(None, "tp", None), P("tp", None, None), P("tp"))
    return jax.shard_map(local, mesh=mesh, in_specs=in_specs, out_specs=P(("seq", "tp"), None), check_vma=False)
```

```python
import jax
import jax.numpy as jnp
import numpy as np
from jax import lax
from jax.experimental import pallas as pl
from jax.experimental.pallas import tpu as pltpu
from jax.sharding import PartitionSpec as P

BLOCK = 128
WMAX = 4
NX, NY, NZ = 4, 4, 8
N_TP = 8
EPS = 1e-06
SCALE = 12.0
bf16, f32 = jnp.bfloat16, jnp.float32


def pairs(move):
    out = []
    for x in range(NX):
        for h in range(2):
            for y in range(NY):
                for z in range(NZ):
                    for c in range(2):
                        to = move(x, h, y, z, c)
                        if to is not None:
                            tx, th, ty, tz, tc = to
                            source = ((y * NZ + z) * 2 + c) * N_TP + x * 2 + h
                            target = ((ty * NZ + tz) * 2 + tc) * N_TP + (tx % NX) * 2 + th
                            out.append((source, target))
    return out


def send(value, move):
    return lax.ppermute(value, ("seq", "tp"), pairs(move))


def to_x(steps):
    return lambda x, h, y, z, c: (x + steps, h, y, z, c)


def to_half(x, h, y, z, c):
    return (x, 1 - h, y, z, c)


def to_core(x, h, y, z, c):
    return (x, h, y, z, 1 - c)


def to_z(flip):
    return lambda x, h, y, z, c: (x, h, y, z ^ flip, c)


def to_y(steps):
    return lambda x, h, y, z, c: (x, h, y + steps, z, c) if y + steps < NY else None


def to_next(x, h, y, z, c):
    place = (y * NZ + z) * 2 + c + 1
    if place == NY * NZ * 2:
        return None
    return (x, h, place // (2 * NZ), place // 2 % NZ, place % 2)


ROWS = 160
VMEM = pl.BlockSpec(memory_space=pltpu.VMEM)
HBM = pl.BlockSpec(memory_space=pltpu.HBM)
SMEM = pl.BlockSpec(memory_space=pltpu.SMEM)


def feature_maps(feat_dim, heads):
    width = heads * 2 * feat_dim
    tables = np.zeros((heads, 4, ROWS, 2 * width), np.float32)
    at = 0
    for i in range(feat_dim):
        for j in range(i, feat_dim):
            for head in range(heads):
                query, key = head * 2 * feat_dim, (head * 2 + 1) * feat_dim
                tables[head, 0, at, query + i] = 1.0 / 32.0 if i == j else 1.0 / 16.0
                tables[head, 1, at, query + j] = 1.0
                tables[head, 2, at, key + i] = 1.0
                tables[head, 3, at, key + j] = 1.0
            at += 1
    for i in range(feat_dim):
        for head in range(heads):
            query, key = head * 2 * feat_dim, (head * 2 + 1) * feat_dim
            tables[head, 0, at, query + i] = 0.25
            tables[head, 2, at, key + i] = 1.0
        tables[:, 1::2, at, width] = 1.0
        at += 1
    tables[:, :, at, width] = 1.0
    return tables


def dot(a, b):
    return jnp.dot(a, b, preferred_element_type=f32)


def dot_t(a, b):
    return lax.dot_general(a, b, (((1,), (1,)), ((), ())), preferred_element_type=f32)


def unit(v):
    return v * lax.rsqrt(jnp.mean(v * v, axis=-1, keepdims=True) + EPS)


def halves(v):
    high = v.astype(bf16)
    return high, (v - high.astype(f32)).astype(bf16)


def position():
    seq, tp = lax.axis_index("seq"), lax.axis_index("tp")
    return lax.div(tp, 2), lax.rem(tp, 2), lax.rem(seq, 2), seq


def contract(parts, wf, ww, mine):
    x, half, _, _ = position()
    side = half if mine else 1 - half
    width = parts[0].shape[1]
    head = ww.shape[2] // 3
    tokens = jnp.concatenate([part[...] for part in parts], axis=1)
    owners = [lax.rem(x + NX - s, NX) * 2 + side for s in (0, 1, 3, 2)]
    rows = [pl.ds(pl.multiple_of(owner * width, width), width) for owner in owners]

    def columns(kind):
        cols = slice(kind * head, (kind + 1) * head)
        weight = [jnp.concatenate([ww[h, r, cols] for h in range(2)], axis=1) for r in rows]
        return dot(tokens, jnp.concatenate(weight, axis=0))

    return dot_t(tokens, jnp.concatenate([wf[:, r] for r in rows], axis=1)), columns


def own_kernel(*refs):
    parts = refs[:NX]
    wf, ww, feats_ref, sums_ref = refs[NX:]
    feats, columns = contract(parts, wf, ww, True)
    feats_ref[...] = feats
    for kind in range(3):
        sums_ref[kind] = columns(kind)


def project_kernel(*refs):
    parts = refs[:NX]
    wf, ww, table, own_feats, own_sums, qf_ref, kv_ref, tail_ref, mine_ref, short_ref, other_ref, qf, tail, sems = refs[NX:]
    core = position()[2]
    head = ww.shape[2] // 3
    feats, columns = contract(parts, wf, ww, False)
    feats = (feats + own_feats[...]).astype(bf16)
    ones = lax.broadcasted_iota(jnp.int32, feats.shape, 1) == 0
    feats = jnp.concatenate([feats, jnp.where(ones, 1.0, 0.0).astype(bf16)], axis=1)
    qf[:, 2 * head :] = feats
    first_tail = kv_ref.shape[0] - tail.shape[0]
    leave = [pltpu.make_async_copy(tail, tail_ref, sems.at[0]), pltpu.make_async_copy(qf, qf_ref, sems.at[1])]
    for kind in (2, 1, 0):
        out = (columns(kind) + own_sums[kind]).astype(bf16)
        if kind == 2:
            values = out
            kv_ref[:, 2 * head :] = out
            tail[:, 2 * head :] = out[first_tail:]
            continue
        for h in range(2):
            cols = slice(h * head, (h + 1) * head)
            normed = unit(out[:, cols].astype(f32)).astype(bf16)
            if kind == 1:
                kv_ref[:, cols] = normed
                tail[:, cols] = normed[first_tail:]
            else:
                qf[:, cols] = normed
        leave[1 - kind].start()
    states = []
    for h in range(2):
        left = dot_t(table[h, 2], feats)
        right = dot_t(table[h, 3], feats)
        high, low = halves(left * right)
        v = values[:, h * head : (h + 1) * head]
        states.append(dot(high, v) + dot(low, v))
    mine = jnp.where(core == 0, states[0], states[1])
    mine_ref[...] = mine
    short_ref[...] = mine.astype(bf16)
    other_ref[...] = jnp.where(core == 0, states[1], states[0]).astype(bf16)
    for copy in leave:
        copy.wait()


def near_kernel(qf_ref, kv_ref, table, near_ref, map_ref, qn_ref, sem):
    copy = pltpu.make_async_copy(qf_ref, qn_ref, sem)
    copy.start()
    copy.wait()
    rows = qn_ref.shape[0]
    heads = near_ref.shape[1] // 128
    head = 128
    feats = qn_ref[:, heads * head :]
    feat = feats.shape[1] // (4 * heads)
    row = lax.broadcasted_iota(jnp.int32, (BLOCK, BLOCK), 0)
    col = lax.broadcasted_iota(jnp.int32, (BLOCK, BLOCK), 1)
    for h in range(heads):
        cols = slice(h * head, (h + 1) * head)
        vcols = slice((heads + h) * head, (heads + h + 1) * head)
        left = dot_t(feats, table[h, 0])
        right = dot_t(feats, table[h, 1])
        map_ref[h] = (left * right).astype(bf16)
        key = lax.broadcasted_iota(jnp.int32, (feats.shape[1], feats.shape[1]), 0)
        lane = lax.broadcasted_iota(jnp.int32, (feats.shape[1], feats.shape[1]), 1)
        first = h * 2 * feat
        moved = (lane == key + feat) & (key >= first) & (key < first + feat)
        query = dot(feats, jnp.where(moved, 1.0, 0.0).astype(bf16)).astype(bf16)
        for b in range(rows // BLOCK):
            at = slice(b * BLOCK, (b + 1) * BLOCK)
            ahead = (b + 1) * BLOCK
            inner = dot_t(query[at], feats[:ahead])
            pair = 1.0 + inner * (0.25 + inner * (1.0 / 32.0))
            last = jnp.where(col <= row, pair[:, b * BLOCK :], 0.0)
            pair = jnp.concatenate([pair[:, : b * BLOCK], last], axis=1) if b else last
            near_ref[at, cols] = dot(pair.astype(bf16), kv_ref[:ahead, vcols])


def window_kernel(win, qf_ref, kv_ref, halo_ref, win_ref, qn_ref, sem):
    copy = pltpu.make_async_copy(qf_ref, qn_ref, sem)
    copy.start()
    copy.wait()
    seq = position()[3]
    rows = qn_ref.shape[0]
    heads = win_ref.shape[1] // 128
    head = 128
    halo = halo_ref.shape[0]
    span = halo + BLOCK
    blocks = rows // BLOCK
    row = lax.broadcasted_iota(jnp.int32, (BLOCK, span), 0)
    col = lax.broadcasted_iota(jnp.int32, (BLOCK, span), 1)
    causal = col <= row + halo
    for h in range(heads):
        cols = slice(h * head, (h + 1) * head)
        vcols = slice((heads + h) * head, (heads + h + 1) * head)
        keys = jnp.concatenate([halo_ref[:, cols], kv_ref[:, cols]], axis=0)
        values = jnp.concatenate([halo_ref[:, vcols], kv_ref[:, vcols]], axis=0)
        for b in range(blocks):
            at = slice(b * BLOCK, (b + 1) * BLOCK)
            scores = dot_t(qn_ref[at, cols], keys[b * BLOCK : b * BLOCK + span]) * (SCALE / head)
            least = jnp.maximum(span // BLOCK - win[h], span // BLOCK - 1 - (seq * blocks + b))
            allowed = causal & (col >= least * BLOCK)
            weights = jnp.where(allowed, jnp.exp(scores), 0.0).astype(bf16)
            win_ref[at, cols] = unit(dot(weights, values[b * BLOCK : b * BLOCK + span]))


def hidden_kernel(ours, theirs, near_ref, win_ref, map_ref, keep_ref, away_ref, hidden):
    x, half, core, _ = position()
    mine, other = ours[...], theirs[...].astype(f32)
    head = mine.shape[1]
    rows = hidden.shape[1]
    for h in range(2):
        cols = slice(h * head, (h + 1) * head)
        state_high, state_low = halves(jnp.where(core == h, mine, other))
        far = dot(map_ref[h], state_high) + dot(map_ref[h], state_low)
        out = (unit(near_ref[:, cols] + far) + win_ref[:, cols]).astype(bf16)
        for g in range(N_TP):
            hidden[g, :, cols] = out[g * rows : (g + 1) * rows]
    for s in range(NX):
        group = lax.rem(x + s, NX) * 2
        keep_ref[s * rows : (s + 1) * rows] = hidden[group + half]
        away_ref[s * rows : (s + 1) * rows] = hidden[group + 1 - half]


def product_kernel(hidden_ref, w_ref, *outs):
    rows = outs[0].shape[0]
    product = dot(hidden_ref[...], w_ref[...]).astype(bf16)
    for s, out in enumerate(outs):
        out[...] = product[s * rows : (s + 1) * rows]


def prefix(mine, short, other, place, beside, attend):
    x, h, y, z, c = place
    across = send(other, lambda x, h, y, z, c: (x, h, y, z ^ 1, 1 - c)).astype(f32)
    beyond = send(short, to_z(1)).astype(f32)
    got = send(other, to_core).astype(f32)
    total = mine + got + across + beyond
    add = (jnp.where(c == 0, mine, 0.0), jnp.where(c == 1, got, 0.0))
    before = jnp.where(z % 2 == 1, across + beyond, 0.0)
    total, before, add = lax.optimization_barrier((total, before, add))
    done = None
    for flip in (2, 4):
        part = send(total.astype(bf16), to_z(flip))
        if flip == 4:
            *behind, halo = done
            part, *behind = lax.optimization_barrier((part, *behind))
        part = part.astype(f32)
        before = before + jnp.where((z ^ flip) < z, part, 0.0)
        total, before = lax.optimization_barrier((total + part, before))
        if flip == 2:
            done = beside(total)
    short = total.astype(bf16)
    earlier = [send(short, to_y(steps)) for steps in (1, 2, 3)]
    *earlier, attended = lax.optimization_barrier((*earlier, attend(halo)))
    for part in earlier:
        before = before + part.astype(f32)
    theirs = send((before + add[0]).astype(bf16), to_core)
    ours = before + add[1]
    return ours, theirs, behind, attended


def shape(dims, kind):
    return jax.ShapeDtypeStruct(dims, kind)


def own_products(parts, wf, ww):
    tok_rows = parts[0].shape[0]
    return pl.pallas_call(
        own_kernel,
        out_shape=(shape((tok_rows, wf.shape[0]), f32), shape((3, tok_rows, 2 * ww.shape[2] // 3), f32)),
        in_specs=[VMEM] * (NX + 2),
        out_specs=(VMEM,) * 2,
        name="own",
        compiler_params=pltpu.CompilerParams(vmem_limit_bytes=LIMIT),
    )(*parts, wf, ww)


def project(parts, wf, ww, tables, own):
    tok_rows = parts[0].shape[0]
    wide = 2 * ww.shape[2] // 3
    queries = shape((tok_rows, wide + 2 * wf.shape[0]), bf16)
    tail = shape(((WMAX - 1) * BLOCK, 2 * wide), bf16)
    return pl.pallas_call(
        project_kernel,
        out_shape=(
            queries,
            shape((tok_rows, 2 * wide), bf16),
            tail,
            shape((ROWS, wide // 2), f32),
            shape((ROWS, wide // 2), bf16),
            shape((ROWS, wide // 2), bf16),
        ),
        in_specs=[VMEM] * (NX + 5),
        out_specs=(HBM, VMEM, HBM, VMEM, VMEM, VMEM),
        scratch_shapes=[
            pltpu.VMEM(queries.shape, bf16),
            pltpu.VMEM(tail.shape, bf16),
            pltpu.SemaphoreType.DMA((2,)),
        ],
        name="project",
        compiler_params=pltpu.CompilerParams(vmem_limit_bytes=LIMIT),
    )(*parts, wf, ww, tables.astype(bf16), *own)


def near(qf, kv, tables):
    tok_rows, wide = kv.shape[0], kv.shape[1] // 2
    return pl.pallas_call(
        near_kernel,
        out_shape=(
            shape((tok_rows, wide), f32),
            shape((2, tok_rows, ROWS), bf16),
        ),
        in_specs=[HBM, VMEM, VMEM],
        out_specs=(VMEM,) * 2,
        scratch_shapes=[pltpu.VMEM(qf.shape, bf16), pltpu.SemaphoreType.DMA],
        name="near",
        compiler_params=pltpu.CompilerParams(vmem_limit_bytes=LIMIT),
    )(qf, kv, tables.astype(bf16))


def window(win_blocks, qf, kv, halo):
    return pl.pallas_call(
        window_kernel,
        out_shape=shape((kv.shape[0], kv.shape[1] // 2), f32),
        in_specs=[SMEM, HBM, VMEM, VMEM],
        out_specs=VMEM,
        scratch_shapes=[pltpu.VMEM(qf.shape, bf16), pltpu.SemaphoreType.DMA],
        name="window",
        compiler_params=pltpu.CompilerParams(vmem_limit_bytes=LIMIT),
    )(win_blocks, qf, kv, halo)


def hidden_rows(ours, theirs, near_out, win_out, query_map):
    tok_rows, wide = near_out.shape
    return pl.pallas_call(
        hidden_kernel,
        out_shape=(shape((tok_rows // 2, wide), bf16),) * 2,
        in_specs=[VMEM] * 5,
        out_specs=(VMEM,) * 2,
        scratch_shapes=[pltpu.VMEM((N_TP, tok_rows // N_TP, wide), bf16)],
        name="hidden",
        compiler_params=pltpu.CompilerParams(vmem_limit_bytes=LIMIT),
    )(ours, theirs, near_out, win_out, query_map)


def product(hidden, w_out):
    return pl.pallas_call(
        product_kernel,
        out_shape=(shape((hidden.shape[0] // NX, w_out.shape[1]), bf16),) * NX,
        in_specs=[VMEM] * 2,
        out_specs=(VMEM,) * NX,
        name="product",
        compiler_params=pltpu.CompilerParams(vmem_limit_bytes=LIMIT),
    )(hidden, w_out)


LIMIT = 12 * 2**20


def local(tokens, w_feature, w_window, w_out, win_blocks):
    model_width, head_count = w_feature.shape[:2]
    feat_dim = w_feature.shape[2] // 2
    seq, tp = lax.axis_index("seq"), lax.axis_index("tp")
    x, h, y, z, c = tp // 2, tp % 2, seq // (2 * NZ), seq // 2 % NZ, seq % 2

    other = send(tokens, to_half)
    parts = [tokens] + [send(tokens, to_x(s)) for s in (1, 3, 2)]
    w_out = w_out.reshape(-1, model_width)
    parts += [other] + [send(other, to_x(s)) for s in (1, 3, 2)]
    tables = feature_maps(feat_dim, head_count)
    wf, ww = w_feature.transpose(1, 2, 0).reshape(-1, model_width), w_window.transpose(1, 0, 2)
    own = own_products(parts[:NX], wf, ww)
    qf, kv, tail, mine, short, theirs = project(parts[NX:], wf, ww, tables, own)

    def beside(total):
        early, kept, _ = lax.optimization_barrier((qf, tail, total))
        return *near(early, kv, tables), send(kept, to_next)

    def attend(halo):
        return window(win_blocks, qf, kv, halo)

    ours, theirs, (near_out, query_map), win_out = prefix(mine, short, theirs, (x, h, y, z, c), beside, attend)
    keep, away = hidden_rows(ours, theirs, near_out, win_out, query_map)

    def summed(total, group):
        for steps in (1, 3, 2):
            total = total + send(group[steps], to_x(steps)).astype(f32)
        return total.astype(bf16)

    group = product(away, w_out)
    away, keep = lax.optimization_barrier((summed(group[0].astype(f32), group), keep))
    group = product(keep, w_out)
    total = lax.optimization_barrier(group[0].astype(f32) + send(away, to_half).astype(f32))
    return summed(total, group)


def solution(mesh):
    in_specs = (P("seq", "tp"), P(None, "tp", None), P(None, "tp", None), P("tp", None, None), P("tp"))
    return jax.shard_map(local, mesh=mesh, in_specs=in_specs, out_specs=P(("seq", "tp"), None), check_vma=False)
```

```python
import jax
import jax.numpy as jnp
import numpy as np
from jax import lax
from jax.experimental import pallas as pl
from jax.experimental.pallas import tpu as pltpu
from jax.sharding import PartitionSpec as P

BLOCK = 128
WMAX = 4
NX, NY, NZ = 4, 4, 8
N_TP = 8
EPS = 1e-06
SCALE = 12.0
bf16, f32 = jnp.bfloat16, jnp.float32


def pairs(move):
    out = []
    for x in range(NX):
        for h in range(2):
            for y in range(NY):
                for z in range(NZ):
                    for c in range(2):
                        to = move(x, h, y, z, c)
                        if to is not None:
                            tx, th, ty, tz, tc = to
                            source = ((y * NZ + z) * 2 + c) * N_TP + x * 2 + h
                            target = ((ty * NZ + tz) * 2 + tc) * N_TP + (tx % NX) * 2 + th
                            out.append((source, target))
    return out


def send(value, move):
    return lax.ppermute(value, ("seq", "tp"), pairs(move))


def to_x(steps):
    return lambda x, h, y, z, c: (x + steps, h, y, z, c)


def to_half(x, h, y, z, c):
    return (x, 1 - h, y, z, c)


def to_core(x, h, y, z, c):
    return (x, h, y, z, 1 - c)


def to_z(flip):
    return lambda x, h, y, z, c: (x, h, y, z ^ flip, c)


def to_y(steps):
    return lambda x, h, y, z, c: (x, h, y + steps, z, c) if y + steps < NY else None


def to_next(x, h, y, z, c):
    place = (y * NZ + z) * 2 + c + 1
    if place == NY * NZ * 2:
        return None
    return (x, h, place // (2 * NZ), place // 2 % NZ, place % 2)


ROWS = 160
VMEM = pl.BlockSpec(memory_space=pltpu.VMEM)
HBM = pl.BlockSpec(memory_space=pltpu.HBM)
SMEM = pl.BlockSpec(memory_space=pltpu.SMEM)


def feature_maps(feat_dim, heads):
    width = heads * 2 * feat_dim
    tables = np.zeros((heads, 4, ROWS, 2 * width), np.float32)
    at = 0
    for i in range(feat_dim):
        for j in range(i, feat_dim):
            for head in range(heads):
                query, key = head * 2 * feat_dim, (head * 2 + 1) * feat_dim
                tables[head, 0, at, query + i] = 1.0 / 32.0 if i == j else 1.0 / 16.0
                tables[head, 1, at, query + j] = 1.0
                tables[head, 2, at, key + i] = 1.0
                tables[head, 3, at, key + j] = 1.0
            at += 1
    for i in range(feat_dim):
        for head in range(heads):
            query, key = head * 2 * feat_dim, (head * 2 + 1) * feat_dim
            tables[head, 0, at, query + i] = 0.25
            tables[head, 2, at, key + i] = 1.0
        tables[:, 1::2, at, width] = 1.0
        at += 1
    tables[:, :, at, width] = 1.0
    return tables


def dot(a, b):
    return jnp.dot(a, b, preferred_element_type=f32)


def dot_t(a, b):
    return lax.dot_general(a, b, (((1,), (1,)), ((), ())), preferred_element_type=f32)


def unit(v):
    return v * lax.rsqrt(jnp.mean(v * v, axis=-1, keepdims=True) + EPS)


def halves(v):
    high = v.astype(bf16)
    return high, (v - high.astype(f32)).astype(bf16)


def position():
    seq, tp = lax.axis_index("seq"), lax.axis_index("tp")
    return lax.div(tp, 2), lax.rem(tp, 2), lax.rem(seq, 2), seq


def contract(parts, wf, ww, mine):
    x, half, _, _ = position()
    side = half if mine else 1 - half
    width = parts[0].shape[1]
    head = ww.shape[2] // 3
    tokens = jnp.concatenate([part[...] for part in parts], axis=1)
    owners = [lax.rem(x + NX - s, NX) * 2 + side for s in (0, 1, 3, 2)]
    rows = [pl.ds(pl.multiple_of(owner * width, width), width) for owner in owners]

    def columns(kind):
        cols = slice(kind * head, (kind + 1) * head)
        weight = [jnp.concatenate([ww[h, r, cols] for h in range(2)], axis=1) for r in rows]
        return dot(tokens, jnp.concatenate(weight, axis=0))

    return dot_t(tokens, jnp.concatenate([wf[:, r] for r in rows], axis=1)), columns


def own_kernel(*refs):
    parts = refs[:NX]
    wf, ww, feats_ref, sums_ref = refs[NX:]
    feats, columns = contract(parts, wf, ww, True)
    feats_ref[...] = feats
    for kind in range(3):
        sums_ref[kind] = columns(kind)


def project_kernel(*refs):
    parts = refs[:NX]
    wf, ww, table, own_feats, own_sums, qf_ref, kv_ref, tail_ref, mine_ref, short_ref, other_ref, qf, tail, sems = refs[NX:]
    core = position()[2]
    head = ww.shape[2] // 3
    feats, columns = contract(parts, wf, ww, False)
    feats = (feats + own_feats[...]).astype(bf16)
    ones = lax.broadcasted_iota(jnp.int32, feats.shape, 1) == 0
    feats = jnp.concatenate([feats, jnp.where(ones, 1.0, 0.0).astype(bf16)], axis=1)
    qf[:, 2 * head :] = feats
    first_tail = kv_ref.shape[0] - tail.shape[0]
    leave = [pltpu.make_async_copy(tail, tail_ref, sems.at[0]), pltpu.make_async_copy(qf, qf_ref, sems.at[1])]
    for kind in (2, 1, 0):
        out = (columns(kind) + own_sums[kind]).astype(bf16)
        if kind == 2:
            values = out
            kv_ref[:, 2 * head :] = out
            tail[:, 2 * head :] = out[first_tail:]
            continue
        for h in range(2):
            cols = slice(h * head, (h + 1) * head)
            normed = unit(out[:, cols].astype(f32)).astype(bf16)
            if kind == 1:
                kv_ref[:, cols] = normed
                tail[:, cols] = normed[first_tail:]
            else:
                qf[:, cols] = normed
        leave[1 - kind].start()
    states = []
    for h in range(2):
        left = dot_t(table[h, 2], feats)
        right = dot_t(table[h, 3], feats)
        high, low = halves(left * right)
        v = values[:, h * head : (h + 1) * head]
        states.append(dot(high, v) + dot(low, v))
    mine = jnp.where(core == 0, states[0], states[1])
    mine_ref[...] = mine
    short_ref[...] = mine.astype(bf16)
    other_ref[...] = jnp.where(core == 0, states[1], states[0]).astype(bf16)
    for copy in leave:
        copy.wait()


def near_kernel(qf_ref, kv_ref, table, near_ref, map_ref, qn_ref, sem):
    copy = pltpu.make_async_copy(qf_ref, qn_ref, sem)
    copy.start()
    copy.wait()
    rows = qn_ref.shape[0]
    heads = near_ref.shape[1] // 128
    head = 128
    feats = qn_ref[:, heads * head :]
    feat = feats.shape[1] // (4 * heads)
    row = lax.broadcasted_iota(jnp.int32, (BLOCK, BLOCK), 0)
    col = lax.broadcasted_iota(jnp.int32, (BLOCK, BLOCK), 1)
    for h in range(heads):
        cols = slice(h * head, (h + 1) * head)
        vcols = slice((heads + h) * head, (heads + h + 1) * head)
        left = dot_t(feats, table[h, 0])
        right = dot_t(feats, table[h, 1])
        map_ref[h] = (left * right).astype(bf16)
        key = lax.broadcasted_iota(jnp.int32, (feats.shape[1], feats.shape[1]), 0)
        lane = lax.broadcasted_iota(jnp.int32, (feats.shape[1], feats.shape[1]), 1)
        first = h * 2 * feat
        moved = (lane == key + feat) & (key >= first) & (key < first + feat)
        query = dot(feats, jnp.where(moved, 1.0, 0.0).astype(bf16)).astype(bf16)
        for b in range(rows // BLOCK):
            at = slice(b * BLOCK, (b + 1) * BLOCK)
            ahead = (b + 1) * BLOCK
            inner = dot_t(query[at], feats[:ahead])
            pair = 1.0 + inner * (0.25 + inner * (1.0 / 32.0))
            last = jnp.where(col <= row, pair[:, b * BLOCK :], 0.0)
            pair = jnp.concatenate([pair[:, : b * BLOCK], last], axis=1) if b else last
            near_ref[at, cols] = dot(pair.astype(bf16), kv_ref[:ahead, vcols])


def window_kernel(win, qf_ref, kv_ref, halo_ref, win_ref, qn_ref, sem):
    copy = pltpu.make_async_copy(qf_ref, qn_ref, sem)
    copy.start()
    copy.wait()
    seq = position()[3]
    rows = qn_ref.shape[0]
    heads = win_ref.shape[1] // 128
    head = 128
    halo = halo_ref.shape[0]
    span = halo + BLOCK
    blocks = rows // BLOCK
    row = lax.broadcasted_iota(jnp.int32, (BLOCK, span), 0)
    col = lax.broadcasted_iota(jnp.int32, (BLOCK, span), 1)
    causal = col <= row + halo
    for h in range(heads):
        cols = slice(h * head, (h + 1) * head)
        vcols = slice((heads + h) * head, (heads + h + 1) * head)
        keys = jnp.concatenate([halo_ref[:, cols], kv_ref[:, cols]], axis=0)
        values = jnp.concatenate([halo_ref[:, vcols], kv_ref[:, vcols]], axis=0)
        for b in range(blocks):
            at = slice(b * BLOCK, (b + 1) * BLOCK)
            scores = dot_t(qn_ref[at, cols], keys[b * BLOCK : b * BLOCK + span]) * (SCALE / head)
            least = jnp.maximum(span // BLOCK - win[h], span // BLOCK - 1 - (seq * blocks + b))
            allowed = causal & (col >= least * BLOCK)
            weights = jnp.where(allowed, jnp.exp(scores), 0.0).astype(bf16)
            win_ref[at, cols] = unit(dot(weights, values[b * BLOCK : b * BLOCK + span]))


def hidden_kernel(ours, theirs, near_ref, win_ref, map_ref, w_ref, keep_ref, *refs):
    outs, hidden = refs[:-1], refs[-1]
    x, half, core, _ = position()
    mine, other = ours[...], theirs[...].astype(f32)
    head = mine.shape[1]
    rows = hidden.shape[1]
    for h in range(2):
        cols = slice(h * head, (h + 1) * head)
        state_high, state_low = halves(jnp.where(core == h, mine, other))
        far = dot(map_ref[h], state_high) + dot(map_ref[h], state_low)
        out = (unit(near_ref[:, cols] + far) + win_ref[:, cols]).astype(bf16)
        for g in range(N_TP):
            hidden[g, :, cols] = out[g * rows : (g + 1) * rows]
    for s in range(NX):
        group = lax.rem(x + s, NX) * 2
        keep_ref[s * rows : (s + 1) * rows] = hidden[group + half]
    groups = [hidden[lax.rem(x + s, NX) * 2 + 1 - half] for s in range(NX)]
    product = dot(jnp.concatenate(groups, axis=0), w_ref[...]).astype(bf16)
    for s, out in enumerate(outs):
        out[...] = product[s * rows : (s + 1) * rows]


def product_kernel(hidden_ref, w_ref, *outs):
    rows = outs[0].shape[0]
    product = dot(hidden_ref[...], w_ref[...]).astype(bf16)
    for s, out in enumerate(outs):
        out[...] = product[s * rows : (s + 1) * rows]


def prefix(mine, short, other, place, beside, attend):
    x, h, y, z, c = place
    across = send(other, lambda x, h, y, z, c: (x, h, y, z ^ 1, 1 - c)).astype(f32)
    beyond = send(short, to_z(1)).astype(f32)
    got = send(other, to_core).astype(f32)
    total = mine + got + across + beyond
    add = (jnp.where(c == 0, mine, 0.0), jnp.where(c == 1, got, 0.0))
    before = jnp.where(z % 2 == 1, across + beyond, 0.0)
    total, before, add = lax.optimization_barrier((total, before, add))
    done = None
    for flip in (2, 4):
        part = send(total.astype(bf16), to_z(flip))
        if flip == 4:
            *behind, halo = done
            part, *behind = lax.optimization_barrier((part, *behind))
        part = part.astype(f32)
        before = before + jnp.where((z ^ flip) < z, part, 0.0)
        total, before = lax.optimization_barrier((total + part, before))
        if flip == 2:
            done = beside(total)
    short = total.astype(bf16)
    earlier = [send(short, to_y(steps)) for steps in (1, 2, 3)]
    *earlier, attended = lax.optimization_barrier((*earlier, attend(halo)))
    for part in earlier:
        before = before + part.astype(f32)
    theirs = send((before + add[0]).astype(bf16), to_core)
    ours = before + add[1]
    return ours, theirs, behind, attended


def shape(dims, kind):
    return jax.ShapeDtypeStruct(dims, kind)


def own_products(parts, wf, ww):
    tok_rows = parts[0].shape[0]
    return pl.pallas_call(
        own_kernel,
        out_shape=(shape((tok_rows, wf.shape[0]), f32), shape((3, tok_rows, 2 * ww.shape[2] // 3), f32)),
        in_specs=[VMEM] * (NX + 2),
        out_specs=(VMEM,) * 2,
        name="own",
        compiler_params=pltpu.CompilerParams(vmem_limit_bytes=LIMIT),
    )(*parts, wf, ww)


def project(parts, wf, ww, tables, own):
    tok_rows = parts[0].shape[0]
    wide = 2 * ww.shape[2] // 3
    queries = shape((tok_rows, wide + 2 * wf.shape[0]), bf16)
    tail = shape(((WMAX - 1) * BLOCK, 2 * wide), bf16)
    return pl.pallas_call(
        project_kernel,
        out_shape=(
            queries,
            shape((tok_rows, 2 * wide), bf16),
            tail,
            shape((ROWS, wide // 2), f32),
            shape((ROWS, wide // 2), bf16),
            shape((ROWS, wide // 2), bf16),
        ),
        in_specs=[VMEM] * (NX + 5),
        out_specs=(HBM, VMEM, HBM, VMEM, VMEM, VMEM),
        scratch_shapes=[
            pltpu.VMEM(queries.shape, bf16),
            pltpu.VMEM(tail.shape, bf16),
            pltpu.SemaphoreType.DMA((2,)),
        ],
        name="project",
        compiler_params=pltpu.CompilerParams(vmem_limit_bytes=LIMIT),
    )(*parts, wf, ww, tables.astype(bf16), *own)


def near(qf, kv, tables):
    tok_rows, wide = kv.shape[0], kv.shape[1] // 2
    return pl.pallas_call(
        near_kernel,
        out_shape=(
            shape((tok_rows, wide), f32),
            shape((2, tok_rows, ROWS), bf16),
        ),
        in_specs=[HBM, VMEM, VMEM],
        out_specs=(VMEM,) * 2,
        scratch_shapes=[pltpu.VMEM(qf.shape, bf16), pltpu.SemaphoreType.DMA],
        name="near",
        compiler_params=pltpu.CompilerParams(vmem_limit_bytes=LIMIT),
    )(qf, kv, tables.astype(bf16))


def window(win_blocks, qf, kv, halo):
    return pl.pallas_call(
        window_kernel,
        out_shape=shape((kv.shape[0], kv.shape[1] // 2), f32),
        in_specs=[SMEM, HBM, VMEM, VMEM],
        out_specs=VMEM,
        scratch_shapes=[pltpu.VMEM(qf.shape, bf16), pltpu.SemaphoreType.DMA],
        name="window",
        compiler_params=pltpu.CompilerParams(vmem_limit_bytes=LIMIT),
    )(win_blocks, qf, kv, halo)


def hidden_rows(ours, theirs, near_out, win_out, query_map, w_out):
    tok_rows, wide = near_out.shape
    return pl.pallas_call(
        hidden_kernel,
        out_shape=(shape((tok_rows // 2, wide), bf16),) + (shape((tok_rows // N_TP, w_out.shape[1]), bf16),) * NX,
        in_specs=[VMEM] * 6,
        out_specs=(VMEM,) * (NX + 1),
        scratch_shapes=[pltpu.VMEM((N_TP, tok_rows // N_TP, wide), bf16)],
        name="hidden",
        compiler_params=pltpu.CompilerParams(vmem_limit_bytes=LIMIT),
    )(ours, theirs, near_out, win_out, query_map, w_out)


def product(hidden, w_out):
    return pl.pallas_call(
        product_kernel,
        out_shape=(shape((hidden.shape[0] // NX, w_out.shape[1]), bf16),) * NX,
        in_specs=[VMEM] * 2,
        out_specs=(VMEM,) * NX,
        name="product",
        compiler_params=pltpu.CompilerParams(vmem_limit_bytes=LIMIT),
    )(hidden, w_out)


LIMIT = 12 * 2**20


def local(tokens, w_feature, w_window, w_out, win_blocks):
    model_width, head_count = w_feature.shape[:2]
    feat_dim = w_feature.shape[2] // 2
    seq, tp = lax.axis_index("seq"), lax.axis_index("tp")
    x, h, y, z, c = tp // 2, tp % 2, seq // (2 * NZ), seq // 2 % NZ, seq % 2

    other = send(tokens, to_half)
    parts = [tokens] + [send(tokens, to_x(s)) for s in (1, 3, 2)]
    w_out = w_out.reshape(-1, model_width)
    parts += [other] + [send(other, to_x(s)) for s in (1, 3, 2)]
    tables = feature_maps(feat_dim, head_count)
    wf, ww = w_feature.transpose(1, 2, 0).reshape(-1, model_width), w_window.transpose(1, 0, 2)
    own = own_products(parts[:NX], wf, ww)
    qf, kv, tail, mine, short, theirs = project(parts[NX:], wf, ww, tables, own)

    def beside(total):
        early, kept, _ = lax.optimization_barrier((qf, tail, total))
        return *near(early, kv, tables), send(kept, to_next)

    def attend(halo):
        return window(win_blocks, qf, kv, halo)

    ours, theirs, (near_out, query_map), win_out = prefix(mine, short, theirs, (x, h, y, z, c), beside, attend)
    keep, *group = hidden_rows(ours, theirs, near_out, win_out, query_map, w_out)

    def summed(total, group):
        for steps in (1, 3, 2):
            total = total + send(group[steps], to_x(steps)).astype(f32)
        return total.astype(bf16)

    away, keep = lax.optimization_barrier((summed(group[0].astype(f32), group), keep))
    group = product(keep, w_out)
    total = lax.optimization_barrier(group[0].astype(f32) + send(away, to_half).astype(f32))
    return summed(total, group)


def solution(mesh):
    in_specs = (P("seq", "tp"), P(None, "tp", None), P(None, "tp", None), P("tp", None, None), P("tp"))
    return jax.shard_map(local, mesh=mesh, in_specs=in_specs, out_specs=P(("seq", "tp"), None), check_vma=False)
```
